256 devices in a mesh: dom: 16 (over x, y), orb: 16 (over z, core).
Axes of the slice: x: 4, y: 4, z: 8, core: 2. Of those that a mesh axis runs over, the one named last changes fastest.
Arguments:
- orbitals: float32 [256, 128, 16, 128], P('orb', 'dom'), may hold values from -6 to 6
- potential: float32 [128, 16, 128], P('dom'), may hold values from 0.2 to 17, as said below
- rotation: float32 [256, 256], P('orb'), may hold values from -0.6 to 0.6
- block: int32 [1], replicated, may hold values from 0 to 15
- owner: int32 [1], replicated, may hold values from 0 to 15
Outputs:
- gradient: float32 [16, 128, 16, 128], P(None, 'dom')
- updated: float32 [256, 128, 16, 128], P('orb', 'dom')
The draws below stay inside these ranges and needn't reach their ends.
Inputs may be any that keep to these rules, and one draw needn't show every extreme that they name: A positive local potential.
All inputs are finite; a program needn't handle non-finite values.
Results may differ from the reference program's by a relative error of at most 0.00017.
Values sent between devices are 32-bit elements; how exact they have to be, the bound alone decides.
A program may use at most 128 MiB of HBM per device.

```python
import jax
import jax.numpy as jnp
from jax import lax

NB = 16
NY = 16
NZ = 128
NX = 128
ORBS = 256
N_ORB = 16


def draw_potential(key, part):
    key = jax.random.fold_in(key, 5)
    ramp_pos = jnp.arange(NX, dtype=jnp.float32)[:, None, None] / NX
    rough = jax.random.uniform(key, (NX, NY, NZ), jnp.float32, 0.5, 1.5)
    values = rough * (1.0 + 5.0 * ramp_pos)
    return values.astype(jnp.float32)


def block_levels(rng, shape, split, low, high):
    factor_of = 1.0
    for position, blocks in split:
        draws = jax.random.uniform(jax.random.fold_in(jax.random.fold_in(rng, 6), position), (blocks,), jnp.float32, low / len(split), high / len(split))
        factor_of = factor_of * jnp.repeat(jnp.exp(draws), shape[position] // blocks).reshape((-1,) + (1,) * (len(shape) - 1 - position))
    return factor_of


def normal_values(rng, shape, deviation, reach, pieces=(), held_as=jnp.bfloat16):
    entries = deviation * jax.random.normal(rng, shape, jnp.float32)
    if pieces:
        entries = entries * block_levels(rng, shape, pieces, -0.22, 0.18)
    return jnp.clip(entries, -reach, reach).astype(held_as)


def setup_inputs(seed: int = 0) -> dict:
    splits = jax.random.split(jax.random.key(seed), 6)
    orbitals = normal_values(splits[0], (ORBS, NX, NY, NZ), 1.0, 6.0, ((0, 16), (1, 16)), jnp.float32)
    potential = draw_potential(jax.random.fold_in(splits[5], 71), 0)
    rotation = normal_values(splits[2], (ORBS, ORBS), 0.1, 0.6, ((0, 16),), jnp.float32)
    block = jax.random.randint(splits[3], (1,), 0, N_ORB).astype(jnp.int32)
    owner = jax.random.randint(splits[4], (1,), 0, N_ORB).astype(jnp.int32)
    return dict(orbitals=orbitals, potential=potential, rotation=rotation, block=block, owner=owner)


CENTER = -5369.0 / 1800.0
SIDES = (12.0 / 7.0, -15.0 / 56.0, 10.0 / 189.0, -1.0 / 112.0, 2.0 / 1925.0, -1.0 / 16632.0)


def kinetic(field):
    summed = 3.0 * CENTER * field
    for offset in range(1, 7):
        weight = SIDES[offset - 1]
        for axis_pos in (1, 2, 3):
            summed = summed + weight * (jnp.roll(field, offset, axis_pos) + jnp.roll(field, -offset, axis_pos))
    return -0.5 * summed


def reference(orbitals, potential, rotation, block, owner):
    nblocks = ORBS // NB
    volume = 1.0 / (NX * NY * NZ)
    start = (block[0] * NB).astype(jnp.int32)
    active = lax.dynamic_slice_in_dim(orbitals, start, NB, 0)
    applied = kinetic(active) + potential[None] * active
    grouped = orbitals.reshape(nblocks, NB, NX, NY, NZ)
    proj = jnp.einsum("jaxyz,cxyz->jac", grouped, applied, precision=lax.Precision.HIGHEST) * volume
    removed = jnp.einsum("jaxyz,jac->cxyz", grouped, proj, precision=lax.Precision.HIGHEST)
    gradient = applied - removed
    panel_start = (owner[0] * NB).astype(jnp.int32)
    panel = lax.dynamic_slice_in_dim(rotation, panel_start, NB, 0)
    coeffs = panel.reshape(NB, nblocks, NB)
    added = jnp.einsum("cxyz,cja->jaxyz", gradient, coeffs, precision=lax.Precision.HIGHEST)
    updated = orbitals + added.reshape(ORBS, NX, NY, NZ)
    return gradient, updated
```

```python
import functools

import jax
import jax.numpy as jnp
from jax import lax
from jax.experimental import pallas as pl
from jax.experimental.pallas import tpu as pltpu
from jax.sharding import PartitionSpec as P

CENTER = -5369.0 / 1800.0
SIDES = (12.0 / 7.0, -15.0 / 56.0, 10.0 / 189.0, -1.0 / 112.0, 2.0 / 1925.0, -1.0 / 16632.0)

MESH = pl.DeviceIdType.MESH
NB = 16
NX, NY, NZ = 8, 16, 128
NDOM, NORB, NCHIP = 16, 16, 8
HALO = 6
LO, HI, ALL = (0, 4), (4, 4), (0, 8)
BF = jnp.bfloat16
F32 = jnp.float32


def split(value):
    high = value.astype(BF)
    return high, (value - high.astype(F32)).astype(BF)


def dot_nt(a, b):
    return lax.dot_general(a, b, (((1,), (1,)), ((), ())), preferred_element_type=F32)


def dot_nn(a, b):
    return lax.dot_general(a, b, (((1,), (0,)), ((), ())), preferred_element_type=F32)


def exact_dot(a, b):
    return lax.dot_general(
        a, b, (((1,), (0,)), ((), ())), preferred_element_type=F32, precision=lax.Precision.HIGHEST
    )


def indicator(shape, row_of, col_of):
    rows = lax.broadcasted_iota(jnp.int32, shape, 0)
    cols = lax.broadcasted_iota(jnp.int32, shape, 1)
    return row_of(rows) == col_of(cols)


def kernel(
    block_ref, owner_ref, x_hbm, pot_hbm, rot_hbm, grad_hbm, upd_hbm,
    x2, xh, xl, pot, rot, mask, remo, act, ham, amat, grad, upd, pbuf, panels,
    a1, a2, d1, b2, sb, send, recv, loc,
):
    dom = lax.axis_index("dom")
    orb = lax.axis_index("orb")
    z = lax.div(orb, 2)
    q = lax.rem(orb, 2)

    def chip(k):
        return lax.rem(z + (k + NCHIP), NCHIP)

    def peer(k):
        return (dom, 2 * chip(k) + q)

    def side(k):
        return (lax.rem(dom + (k + NDOM), NDOM), orb)

    sibling = (dom, orb + 1 - 2 * q)
    sems = iter(range(send.shape[0]))
    started = []

    def remote(src, dst, device):
        i = next(sems)
        copy = pltpu.make_async_remote_copy(
            src_ref=src, dst_ref=dst, send_sem=send.at[i], recv_sem=recv.at[i],
            device_id=device, device_id_type=MESH,
        )
        copy.start()
        started.append(copy)
        return copy

    load_x = pltpu.make_async_copy(x_hbm, x2.at[q], loc.at[0])
    load_pot = pltpu.make_async_copy(pot_hbm, pot, loc.at[1])
    load_rot = pltpu.make_async_copy(rot_hbm, rot, loc.at[2])
    for copy in (load_x, load_pot, load_rot):
        copy.start()
    barrier = pltpu.get_barrier_semaphore()
    for k in range(1, NDOM):
        pl.semaphore_signal(barrier, inc=1, device_id=side(k), device_id_type=MESH)
    for k in range(1, NORB):
        pl.semaphore_signal(
            barrier, inc=1, device_id=(dom, lax.rem(orb + k, NORB)), device_id_type=MESH
        )
    for copy in (load_x, load_pot, load_rot):
        copy.wait()
    pl.semaphore_wait(barrier, NDOM + NORB - 2)

    twin = []
    for parity in (1 - q, q):
        twin.append([
            remote(x2.at[q, 2 * s + parity], x2.at[q, 2 * s + parity], sibling)
            for s in range(NCHIP)
        ])

    def reduce_scatter(part, slot):
        def cut(ref, *lead, half=ALL):
            return ref.at[(*lead, pl.ds(*half))]

        def first(sign, half):
            src = cut(part, chip(3 * sign), half=half)
            return remote(src, cut(a1, slot, (1 - sign) // 2, half=half), peer(sign))

        def far(sign, half):
            return remote(cut(part, chip(4), half=half), a2.at[slot, (1 - sign) // 2], peer(2 * sign))

        def near(sign):
            return remote(part.at[chip(sign)], d1.at[slot, (1 - sign) // 2], peer(sign))

        def second(sign, half, arrivals, with_far):
            i = (1 - sign) // 2
            for copy in arrivals:
                copy.wait_recv()
            rows = slice(half[0], half[0] + half[1])
            total = part[chip(2 * sign), rows] + a1[slot, i, rows]
            if with_far:
                total = total + a2[slot, i]
            sb[slot, i, rows] = total
            return remote(
                cut(sb, slot, i, half=half), cut(b2, slot, i, half=half), peer(2 * sign)
            )

        p_hi, m_lo = first(1, HI), first(-1, LO)
        p_far, m_far = far(1, LO), far(-1, HI)
        p_lo, m_hi = first(1, LO), first(-1, HI)
        nears = [near(1), near(-1)]
        last = [
            second(1, HI, [p_hi], False),
            second(-1, LO, [m_lo], False),
            second(1, LO, [p_far, p_lo], True),
            second(-1, HI, [m_far, m_hi], True),
        ]
        for copy in nears + last:
            copy.wait_recv()
        return part[z] + (d1[slot, 0] + d1[slot, 1]) + (b2[slot, 0] + b2[slot, 1])

    def all_gather(buf, index, arrived=lambda k: None):
        def forward(k, half, to):
            ref = buf.at[index(k), pl.ds(*half)]
            return remote(ref, ref, peer(to))

        p_lo, m_hi = forward(0, LO, 2), forward(0, HI, -2)
        p_hi, m_lo = forward(0, HI, 2), forward(0, LO, -2)
        p_near, m_near = forward(0, ALL, 1), forward(0, ALL, -1)
        arrived(0)
        p_lo.wait_recv()
        p_far, p_3lo = forward(-2, LO, 2), forward(-2, LO, 1)
        m_hi.wait_recv()
        m_far, m_3hi = forward(2, HI, -2), forward(2, HI, -1)
        p_hi.wait_recv()
        p_3hi = forward(-2, HI, 1)
        arrived(-2)
        m_lo.wait_recv()
        m_3lo = forward(2, LO, -1)
        arrived(2)
        for k, copies in (
            (-1, (p_near,)), (1, (m_near,)), (-3, (p_3lo, p_3hi)), (3, (m_3hi, m_3lo)), (4, (p_far, m_far)),
        ):
            for copy in copies:
                copy.wait_recv()
            arrived(k)

    block = block_ref[0]
    root_chip = lax.div(block, 2)
    root_core = lax.rem(block, 2)
    is_root = root_chip == z
    for copy in twin[0]:
        copy.wait_recv()
    for s in range(NCHIP):
        mine = jnp.where(root_core == 0, x2[0, 2 * s + q], x2[1, 2 * s + q])
        mask[s] = jnp.where(is_root, mine, 0.0)
    act[pl.ds(HALO, NX)] = reduce_scatter(mask, 0)

    up = remote(act.at[pl.ds(NX, HALO)], act.at[pl.ds(0, HALO)], side(1))
    down = remote(act.at[pl.ds(HALO, HALO)], act.at[pl.ds(HALO + NX, HALO)], side(-1))

    half = pl.ds(pl.multiple_of(lax.div(orb, 8) * 128, 128), 128)
    panel_copies = []
    for k in range(1, NORB):
        to = lax.rem(orb + k, NORB)
        cols = pl.ds(pl.multiple_of(lax.div(to, 8) * 128, 128), 128)
        panel_copies.append(remote(rot.at[:, cols], panels.at[orb], (dom, to)))
    panels[orb] = rot[:, half]

    field = act[pl.ds(HALO, NX)]
    inner = (pot[...] - 1.5 * CENTER) * field
    for k in range(1, 7):
        near = (
            pltpu.roll(field, k, 1) + pltpu.roll(field, NY - k, 1)
            + pltpu.roll(field, k, 2) + pltpu.roll(field, NZ - k, 2)
        )
        inner = inner - (0.5 * SIDES[k - 1]) * near
    up.wait_recv()
    down.wait_recv()
    for k in range(1, 7):
        inner = inner - (0.5 * SIDES[k - 1]) * (act[pl.ds(HALO + k, NX)] + act[pl.ds(HALO - k, NX)])
    ham[...] = inner
    amat[z] = inner

    for copy in twin[1]:
        copy.wait_recv()
    for j in range(2):
        def cast(a, carry, j=j):
            high, low = split(x2[j, a])
            xh[j, a] = high
            xl[j, a] = low
            return carry
        lax.fori_loop(0, NB, cast, 0)
    all_gather(amat, chip)

    rows, cols = NCHIP * NY, 2 * NB * NY
    same_y = indicator((rows, cols), lambda r: r & (NY - 1), lambda c: c & (NY - 1))
    gram = jnp.zeros((rows, cols), F32)
    for x in range(0, NX, 2):
        a_pair = jnp.concatenate([amat[:, x].reshape(rows, NZ), amat[:, x + 1].reshape(rows, NZ)], 1)
        h_pair, l_pair = (
            jnp.concatenate([r[:, :, x].reshape(cols, NZ), r[:, :, x + 1].reshape(cols, NZ)], 1)
            for r in (xh, xl)
        )
        a_high, a_low = split(a_pair)
        both = dot_nt(jnp.concatenate([a_high, a_low], 0), h_pair)
        gram = gram + (both[:rows] + both[rows:] + dot_nt(a_high, l_pair))
    summed = jnp.where(same_y, gram, 0.0).reshape(NCHIP, NY, cols).sum(1)
    of_orbital = jnp.where(indicator((cols, 128), lambda r: r // NY, lambda c: c), 1.0, 0.0)
    pbuf[dom] = exact_dot(summed, of_orbital)
    exchange = [remote(pbuf.at[dom], pbuf.at[dom], side(k)) for k in range(1, NDOM)]
    for copy in exchange:
        copy.wait_recv()
    proj = pbuf[...].sum(0) * (1.0 / (NX * NDOM * NY * NZ))

    to_rows = jnp.where(indicator((128, cols), lambda r: r, lambda c: c // NY), 1.0, 0.0)
    spread = exact_dot(proj, to_rows)
    spread = jnp.broadcast_to(spread[:, None, :], (NCHIP, NY, cols)).reshape(rows, cols)
    k_high, k_low = split(jnp.where(same_y, spread, 0.0))
    k_both = jnp.concatenate([k_high, k_low], 0)
    for x in range(0, NX, 2):
        h_pair, l_pair = (
            jnp.concatenate([r[:, :, x].reshape(cols, NZ), r[:, :, x + 1].reshape(cols, NZ)], 1)
            for r in (xh, xl)
        )
        both = dot_nn(k_both, h_pair)
        part = both[:rows] + both[rows:] + dot_nn(k_high, l_pair)
        remo[:, x] = part[:, :NZ].reshape(NCHIP, NY, NZ)
        remo[:, x + 1] = part[:, NZ:].reshape(NCHIP, NY, NZ)
    grad[orb] = ham[...] - reduce_scatter(remo, 1)

    twins = []

    def to_sibling(k):
        ref = grad.at[2 * chip(k) + q]
        twins.append(remote(ref, ref, sibling))

    all_gather(grad, lambda k: 2 * chip(k) + q, to_sibling)

    for copy in panel_copies:
        copy.wait_recv()
    panel = panels[owner_ref[0]]
    rows = NB * NY
    same_y = indicator((rows, rows), lambda r: r & (NY - 1), lambda c: c & (NY - 1))
    column = lax.rem(orb, 8) * NB
    of_column = jnp.where(indicator((rows, 128), lambda r: r // NY + column, lambda c: c), 1.0, 0.0)
    by_row = lax.dot_general(
        of_column, panel, (((1,), (1,)), ((), ())), preferred_element_type=F32,
        precision=lax.Precision.HIGHEST,
    )
    to_rows = jnp.where(indicator((NB, rows), lambda r: r, lambda c: c // NY), 1.0, 0.0)
    w_high, w_low = split(jnp.where(same_y, exact_dot(by_row, to_rows), 0.0))
    w_both = jnp.concatenate([w_high, w_low], 0)
    for copy in twins:
        copy.wait_recv()
    out_grad = pltpu.make_async_copy(grad, grad_hbm, loc.at[3])
    out_grad.start()
    outs = []
    for x in range(0, NX, 2):
        g_pair = jnp.concatenate([grad[:, x].reshape(rows, NZ), grad[:, x + 1].reshape(rows, NZ)], 1)
        g_high, g_low = split(g_pair)
        both = dot_nn(w_both, g_high)
        part = both[:rows] + both[rows:] + dot_nn(w_high, g_low)
        upd[:, x] = x2[q, :, x] + part[:, :NZ].reshape(NB, NY, NZ)
        upd[:, x + 1] = x2[q, :, x + 1] + part[:, NZ:].reshape(NB, NY, NZ)
        pair = pl.ds(x, 2)
        copy = pltpu.make_async_copy(upd.at[:, pair], upd_hbm.at[:, pair], loc.at[4 + x // 2])
        copy.start()
        outs.append(copy)
    for copy in started:
        copy.wait_send()
    out_grad.wait()
    for copy in outs:
        copy.wait()


def per_device(orbitals, potential, rotation, block, owner):
    shard = (NX, NY, NZ)
    half = (NX // 2, NY, NZ)
    scratch = [
        pltpu.VMEM((2, NB, *shard), F32),
        pltpu.VMEM((2, NB, *shard), BF),
        pltpu.VMEM((2, NB, *shard), BF),
        pltpu.VMEM(shard, F32),
        pltpu.VMEM((NB, NB * NORB), F32),
        pltpu.VMEM((NCHIP, *shard), F32),
        pltpu.VMEM((NCHIP, *shard), F32),
        pltpu.VMEM((NX + 2 * HALO, NY, NZ), F32),
        pltpu.VMEM(shard, F32),
        pltpu.VMEM((NCHIP, *shard), F32),
        pltpu.VMEM((NB, *shard), F32),
        pltpu.VMEM((NB, *shard), F32),
        pltpu.VMEM((NDOM, NCHIP, 128), F32),
        pltpu.VMEM((NORB, NB, 128), F32),
        pltpu.VMEM((2, 2, *shard), F32),
        pltpu.VMEM((2, 2, *half), F32),
        pltpu.VMEM((2, 2, *shard), F32),
        pltpu.VMEM((2, 2, *shard), F32),
        pltpu.VMEM((2, 2, *shard), F32),
        pltpu.SemaphoreType.DMA((112,)),
        pltpu.SemaphoreType.DMA((112,)),
        pltpu.SemaphoreType.DMA((8,)),
    ]
    smem = pl.BlockSpec(memory_space=pltpu.SMEM)
    hbm = pl.BlockSpec(memory_space=pl.ANY)
    return pl.pallas_call(
        kernel,
        out_shape=(
            jax.ShapeDtypeStruct((NB, *shard), F32),
            jax.ShapeDtypeStruct((NB, *shard), F32),
        ),
        in_specs=[smem, smem, hbm, hbm, hbm],
        out_specs=(hbm, hbm),
        scratch_shapes=scratch,
        compiler_params=pltpu.CompilerParams(
            collective_id=0, has_side_effects=True, vmem_limit_bytes=48 << 20
        ),
        cost_estimate=pl.CostEstimate(flops=1 << 28, bytes_accessed=3 << 20, transcendentals=0),
        name="gradient_update",
    )(block, owner, orbitals, potential, rotation)


def solution(mesh):
    in_specs = (P("orb", "dom", None, None), P("dom", None, None), P("orb", None), P(), P())
    out_specs = (P(None, "dom", None, None), P("orb", "dom", None, None))
    return jax.shard_map(
        per_device, mesh=mesh, in_specs=in_specs, out_specs=out_specs, check_vma=False
    )
```

```python
import functools

import jax
import jax.numpy as jnp
from jax import lax
from jax.experimental import pallas as pl
from jax.experimental.pallas import tpu as pltpu
from jax.sharding import PartitionSpec as P

CENTER = -5369.0 / 1800.0
SIDES = (12.0 / 7.0, -15.0 / 56.0, 10.0 / 189.0, -1.0 / 112.0, 2.0 / 1925.0, -1.0 / 16632.0)

MESH = pl.DeviceIdType.MESH
NB = 16
NX, NY, NZ = 8, 16, 128
NDOM, NORB, NCHIP = 16, 16, 8
HALO = 6
BF = jnp.bfloat16
F32 = jnp.float32


def split(value):
    high = value.astype(BF)
    return high, (value - high.astype(F32)).astype(BF)


def dot_nt(a, b):
    return lax.dot_general(a, b, (((1,), (1,)), ((), ())), preferred_element_type=F32)


def dot_nn(a, b):
    return lax.dot_general(a, b, (((1,), (0,)), ((), ())), preferred_element_type=F32)


def indicator(shape, row_of, col_of):
    rows = lax.broadcasted_iota(jnp.int32, shape, 0)
    cols = lax.broadcasted_iota(jnp.int32, shape, 1)
    return row_of(rows) == col_of(cols)


def kernel(
    block_ref, owner_ref, x_hbm, pot_hbm, rot_hbm, grad_hbm, upd_hbm,
    x2, xh, xl, pot, rot, mask, remo, act, amat, grad, upd, pbuf, packed, panels,
    a1, a2, d1, b2, sb, send, recv, loc,
):
    dom = lax.axis_index("dom")
    orb = lax.axis_index("orb")
    z = lax.div(orb, 2)
    q = lax.rem(orb, 2)

    def chip(k):
        return lax.rem(z + (k + 2 * NCHIP), NCHIP)

    def peer(k):
        return (dom, 2 * chip(k) + q)

    def side(k):
        return (lax.rem(dom + (k + NDOM), NDOM), orb)

    sibling = (dom, orb + 1 - 2 * q)
    sems = iter(range(send.shape[0]))
    started = []

    def remote(src, dst, device):
        i = next(sems)
        copy = pltpu.make_async_remote_copy(
            src_ref=src, dst_ref=dst, send_sem=send.at[i], recv_sem=recv.at[i],
            device_id=device, device_id_type=MESH,
        )
        copy.start()
        started.append(copy)
        return copy

    def arrive(copies):
        for copy in copies:
            copy.wait_recv()

    load_x = pltpu.make_async_copy(x_hbm, x2.at[q], loc.at[0])
    load_pot = pltpu.make_async_copy(pot_hbm, pot, loc.at[1])
    load_rot = pltpu.make_async_copy(rot_hbm, rot, loc.at[2])
    for copy in (load_x, load_pot, load_rot):
        copy.start()
    barrier = pltpu.get_barrier_semaphore()
    for k in range(1, NDOM):
        pl.semaphore_signal(barrier, inc=1, device_id=side(k), device_id_type=MESH)
    for k in range(1, NORB):
        pl.semaphore_signal(
            barrier, inc=1, device_id=(dom, lax.rem(orb + k, NORB)), device_id_type=MESH
        )
    for copy in (load_x, load_pot, load_rot):
        copy.wait()
    pl.semaphore_wait(barrier, NDOM + NORB - 2)

    def scatter_far(part, slot, h):
        whole, front, back = pl.ds(4 * h, 4), pl.ds(4 * h, 2), pl.ds(4 * h + 2, 2)
        return (
            remote(part(4).at[front], a2.at[slot, 0, front], peer(2)),
            remote(part(4).at[back], a2.at[slot, 1, back], peer(-2)),
            remote(part(3).at[whole], a1.at[slot, 0, whole], peer(1)),
            remote(part(-3).at[whole], a1.at[slot, 1, whole], peer(-1)),
        )

    def scatter_mid(part, slot, h, far):
        whole, front, back = pl.ds(4 * h, 4), pl.ds(4 * h, 2), pl.ds(4 * h + 2, 2)
        sent = []
        for i, sign, quarter in ((0, 1, front), (1, -1, back)):
            arrive((far[i], far[2 + i]))
            sb[slot, i, whole] = part(2 * sign)[whole] + a1[slot, i, whole]
            sb[slot, i, quarter] = sb[slot, i, quarter] + a2[slot, i, quarter]
            sent.append(remote(sb.at[slot, i, whole], b2.at[slot, i, whole], peer(2 * sign)))
        return tuple(sent)

    def scatter_near(part, slot, h):
        whole = pl.ds(4 * h, 4)
        return (
            remote(part(1).at[whole], d1.at[slot, 0, whole], peer(1)),
            remote(part(-1).at[whole], d1.at[slot, 1, whole], peer(-1)),
        )

    def scatter_sum(part, slot, h, copies):
        whole = pl.ds(4 * h, 4)
        arrive(copies)
        return (
            part(0)[whole]
            + (d1[slot, 0, whole] + d1[slot, 1, whole])
            + (b2[slot, 0, whole] + b2[slot, 1, whole])
        )

    def give(shard, k, to, planes):
        ref = shard(k).at[planes]
        return remote(ref, ref, peer(to))

    def gather_two(shard, h):
        whole = pl.ds(4 * h, 4)
        return give(shard, 0, 2, whole), give(shard, 0, -2, whole)

    def gather_one(shard, h):
        whole = pl.ds(4 * h, 4)
        return give(shard, 0, 1, whole), give(shard, 0, -1, whole)

    def gather_on(shard, h, two, arrived=lambda k, h: None):
        whole, front, back = pl.ds(4 * h, 4), pl.ds(4 * h, 2), pl.ds(4 * h + 2, 2)
        arrive(two[:1])
        ahead = give(shard, -2, 2, front), give(shard, -2, 1, whole)
        arrived(-2, h)
        arrive(two[1:])
        behind = give(shard, 2, -2, back), give(shard, 2, -1, whole)
        arrived(2, h)
        return ahead + behind

    order = (4, 3, -3, 2, -2, 1, -1, 0)

    def to_twin(k, parity):
        ref = x2.at[q, 2 * chip(k) + parity]
        return remote(ref, ref, sibling)

    wanted = [to_twin(k, 1 - q) for k in order]
    others = [to_twin(k, q) for k in order]

    block = block_ref[0]
    root_core = lax.rem(block, 2)
    is_root = lax.div(block, 2) == z

    def masked(k):
        return mask.at[chip(k)]

    def fill(pairs):
        for k, copy in pairs:
            copy.wait_recv()
            i = 2 * chip(k) + q
            mine = jnp.where(root_core == 0, x2[0, i], x2[1, i])
            mask[chip(k)] = jnp.where(is_root, mine, 0.0)

    pairs = list(zip(order, wanted))
    fill(pairs[:3])
    far = [scatter_far(masked, 0, h) for h in range(2)]
    fill(pairs[3:])
    near = [scatter_near(masked, 0, h) for h in range(2)]
    mid = [scatter_mid(masked, 0, h, far[h]) for h in range(2)]
    for h in range(2):
        act[pl.ds(HALO + 4 * h, 4)] = scatter_sum(masked, 0, h, near[h] + mid[h])

    halo = (
        remote(act.at[pl.ds(NX, HALO)], act.at[pl.ds(0, HALO)], side(1)),
        remote(act.at[pl.ds(HALO, HALO)], act.at[pl.ds(HALO + NX, HALO)], side(-1)),
    )

    r_high, r_low = split(rot[...])
    r_both = jnp.concatenate([r_high, r_low], 0)
    for j in range(0, NORB, 2):
        base = (j // 8) * 128
        shape = (128, 256)
        pick = indicator(
            shape, lambda r: r + base, lambda c: (j + (c >> 7)) * NB + (c & (NB - 1))
        )
        both = dot_nn(r_both[:, base : base + 128], jnp.where(pick, 1.0, 0.0).astype(BF))
        both = both[:NB] + both[NB:]
        own = indicator((NB, 256), lambda r: r & 7, lambda c: (c & 127) >> 4)
        both = jnp.where(own, both, 0.0).reshape(2, 8, 256).sum(1)
        packed[j] = both[:, :128]
        packed[j + 1] = both[:, 128:]
    panels[orb] = packed[orb]
    panel_copies = []
    for k in range(1, NORB):
        to = lax.rem(orb + k, NORB)
        panel_copies.append(remote(packed.at[to], panels.at[orb], (dom, to)))

    field = act[pl.ds(HALO, NX)]
    inner = (pot[...] - 1.5 * CENTER) * field
    for k in range(1, 7):
        near = (
            pltpu.roll(field, k, 1) + pltpu.roll(field, NY - k, 1)
            + pltpu.roll(field, k, 2) + pltpu.roll(field, NZ - k, 2)
        )
        inner = inner - (0.5 * SIDES[k - 1]) * near
    arrive(others)
    for j in range(2):
        def cast(a, carry, j=j):
            high, low = split(x2[j, a])
            xh[j, a] = high
            xl[j, a] = low
            return carry
        lax.fori_loop(0, NB, cast, 0)
    arrive(halo)
    for k in range(1, 7):
        inner = inner - (0.5 * SIDES[k - 1]) * (act[pl.ds(HALO + k, NX)] + act[pl.ds(HALO - k, NX)])
    amat[z] = inner

    cols = 2 * NB * NY

    def shard(k):
        return amat.at[chip(k)]

    def same_y(rows):
        return indicator((rows, cols), lambda r: r & (NY - 1), lambda c: c & (NY - 1))

    def x_pairs():
        for x in range(0, NX, 2):
            yield x, *(
                jnp.concatenate([r[:, :, x].reshape(cols, NZ), r[:, :, x + 1].reshape(cols, NZ)], 1)
                for r in (xh, xl)
            )

    def project(batch, ks):
        rows = len(ks) * NY
        gram = jnp.zeros((rows, cols), F32)
        for x, h_pair, l_pair in x_pairs():
            a_pair = jnp.concatenate([
                jnp.concatenate([shard(k)[x] for k in ks], 0),
                jnp.concatenate([shard(k)[x + 1] for k in ks], 0),
            ], 1)
            a_high, a_low = split(a_pair)
            both = dot_nt(jnp.concatenate([a_high, a_low], 0), h_pair)
            gram = gram + (both[:rows] + both[rows:] + dot_nt(a_high, l_pair))
        summed = jnp.where(same_y(rows), gram, 0.0).reshape(len(ks), NY, cols).sum(1)
        summed = jnp.concatenate([summed, jnp.zeros((8 - len(ks), cols), F32)], 0)
        of_orbital = indicator((cols, 128), lambda r: r >> 4, lambda c: c)
        s_both = jnp.concatenate(split(summed), 0)
        summed = dot_nn(s_both, jnp.where(of_orbital, 1.0, 0.0).astype(BF))
        pbuf[batch, dom] = summed[:8] + summed[8:]
        ref = pbuf.at[batch, dom]
        return [remote(ref, ref, side(k)) for k in range(1, NDOM)]

    def remove(batch, ks, copies, halves):
        rows = len(ks) * NY
        arrive(copies)
        proj = pbuf[batch].sum(0) * (1.0 / (NX * NDOM * NY * NZ))
        to_rows = indicator((128, cols), lambda r: r, lambda c: c >> 4)
        spread = dot_nn(
            jnp.concatenate(split(proj), 0), jnp.where(to_rows, 1.0, 0.0).astype(BF)
        )
        keep = same_y(rows)
        weights = []
        for first in (0, 8):
            one = spread[first : first + len(ks)]
            one = jnp.broadcast_to(one[:, None, :], (len(ks), NY, cols)).reshape(rows, cols)
            weights.append(jnp.where(keep, one, 0.0).astype(BF))
        k_both = jnp.concatenate(weights, 0)
        for x, h_pair, l_pair in x_pairs():
            both = dot_nn(k_both, h_pair)
            part = both[:rows] + both[rows:] + dot_nn(weights[0], l_pair)
            for i, k in enumerate(ks):
                remo[chip(k), x] = part[i * NY : (i + 1) * NY, :NZ]
                remo[chip(k), x + 1] = part[i * NY : (i + 1) * NY, NZ:]
            if x == 2 or x == 6:
                halves(x // 4)

    two = [gather_two(shard, 0)]
    one = [gather_one(shard, 0), gather_one(shard, 1)]
    two.append(gather_two(shard, 1))
    on = [gather_on(shard, 0, two[0])]
    arrive(one[0] + one[1])
    batches = ((0, 1, -1), (2, -2), (3, -3, 4))
    sums = [project(0, batches[0])]
    on.append(gather_on(shard, 1, two[1]))
    sums.append(project(1, batches[1]))

    def removed(k):
        return remo.at[chip(k + 4)]

    def owned(k):
        return grad.at[2 * chip(k + 4) + q]

    far, mid, near, twins = [], [], [], [[], []]
    remove(0, batches[0], sums[0], lambda h: far.append(scatter_far(removed, 1, h)))
    arrive(on[0] + on[1])
    sums.append(project(2, batches[2]))
    remove(1, batches[1], sums[1], lambda h: None)
    mid.append(scatter_mid(removed, 1, 0, far[0]))
    mid.append(scatter_mid(removed, 1, 1, far[1]))
    remove(2, batches[2], sums[2], lambda h: near.append(scatter_near(removed, 1, h)))

    def to_sibling(k, h):
        ref = owned(k).at[pl.ds(4 * h, 4)]
        twins[h].append(remote(ref, ref, sibling))

    two, one, on = [], [], []
    for h in range(2):
        half = pl.ds(4 * h, 4)
        owned(0)[half] = amat[chip(4), half] - scatter_sum(removed, 1, h, near[h] + mid[h])
        two.append(gather_two(owned, h))
        one.append(gather_one(owned, h))
        to_sibling(0, h)

    arrive(panel_copies)
    rows = NB * NY
    panel = panels[owner_ref[0]]
    panel = jnp.broadcast_to(panel[:, None, :], (2, 8, 128)).reshape(NB, 128)
    own = indicator((NB, 128), lambda r: r & 7, lambda c: c >> 4)
    p_both = jnp.concatenate(split(jnp.where(own, panel, 0.0)), 0)
    of_column = indicator((rows, 128), lambda r: r >> 4, lambda c: c & (NB - 1))
    by_row = dot_nt(jnp.where(of_column, 1.0, 0.0).astype(BF), p_both).astype(BF)
    to_rows = indicator((NB, rows), lambda r: r, lambda c: c >> 4)
    to_rows = jnp.where(to_rows, 1.0, 0.0).astype(BF)
    keep = indicator((rows, rows), lambda r: r & (NY - 1), lambda c: c & (NY - 1))
    w_high, w_low = (
        jnp.where(keep, dot_nn(one_of, to_rows), 0.0).astype(BF)
        for one_of in (by_row[:, :NB], by_row[:, NB:])
    )
    w_both = jnp.concatenate([w_high, w_low], 0)

    for h in range(2):
        on.append(gather_on(owned, h, two[h], to_sibling))
    for h in range(2):
        for i, k in ((0, -1), (1, 1)):
            arrive(one[h][i : i + 1])
            to_sibling(k, h)
    outs = []
    for h in range(2):
        arrive(on[h][1:2])
        to_sibling(-3, h)
        arrive(on[h][3:4])
        to_sibling(3, h)
        arrive((on[h][0], on[h][2]))
        to_sibling(4, h)
        arrive(twins[h])
        half = pl.ds(4 * h, 4)
        outs.append(pltpu.make_async_copy(grad.at[:, half], grad_hbm.at[:, half], loc.at[3 + h]))
        outs[-1].start()
        for x in range(4 * h, 4 * h + 4, 2):
            g_pair = jnp.concatenate(
                [grad[:, x].reshape(rows, NZ), grad[:, x + 1].reshape(rows, NZ)], 1
            )
            g_high, g_low = split(g_pair)
            both = dot_nn(w_both, g_high)
            part = both[:rows] + both[rows:] + dot_nn(w_high, g_low)
            upd[:, x] = x2[q, :, x] + part[:, :NZ].reshape(NB, NY, NZ)
            upd[:, x + 1] = x2[q, :, x + 1] + part[:, NZ:].reshape(NB, NY, NZ)
        outs.append(pltpu.make_async_copy(upd.at[:, half], upd_hbm.at[:, half], loc.at[5 + h]))
        outs[-1].start()
    for copy in started:
        copy.wait_send()
    for copy in outs:
        copy.wait()


def per_device(orbitals, potential, rotation, block, owner):
    shard = (NX, NY, NZ)
    scratch = [
        pltpu.VMEM((2, NB, *shard), F32),
        pltpu.VMEM((2, NB, *shard), BF),
        pltpu.VMEM((2, NB, *shard), BF),
        pltpu.VMEM(shard, F32),
        pltpu.VMEM((NB, NB * NORB), F32),
        pltpu.VMEM((NCHIP, *shard), F32),
        pltpu.VMEM((NCHIP, *shard), F32),
        pltpu.VMEM((NX + 2 * HALO, NY, NZ), F32),
        pltpu.VMEM((NCHIP, *shard), F32),
        pltpu.VMEM((NB, *shard), F32),
        pltpu.VMEM((NB, *shard), F32),
        pltpu.VMEM((3, NDOM, 8, 128), F32),
        pltpu.VMEM((NORB, 2, 128), F32),
        pltpu.VMEM((NORB, 2, 128), F32),
        pltpu.VMEM((2, 2, *shard), F32),
        pltpu.VMEM((2, 2, *shard), F32),
        pltpu.VMEM((2, 2, *shard), F32),
        pltpu.VMEM((2, 2, *shard), F32),
        pltpu.VMEM((2, 2, *shard), F32),
        pltpu.SemaphoreType.DMA((160,)),
        pltpu.SemaphoreType.DMA((160,)),
        pltpu.SemaphoreType.DMA((8,)),
    ]
    smem = pl.BlockSpec(memory_space=pltpu.SMEM)
    hbm = pl.BlockSpec(memory_space=pl.ANY)
    return pl.pallas_call(
        kernel,
        out_shape=(
            jax.ShapeDtypeStruct((NB, *shard), F32),
            jax.ShapeDtypeStruct((NB, *shard), F32),
        ),
        in_specs=[smem, smem, hbm, hbm, hbm],
        out_specs=(hbm, hbm),
        scratch_shapes=scratch,
        compiler_params=pltpu.CompilerParams(
            collective_id=0, has_side_effects=True, vmem_limit_bytes=48 << 20
        ),
        cost_estimate=pl.CostEstimate(flops=1 << 28, bytes_accessed=3 << 20, transcendentals=0),
        name="gradient_update",
    )(
        block, owner,
        *(pltpu.with_memory_space_constraint(v, pltpu.HBM) for v in (orbitals, potential, rotation)),
    )


def solution(mesh):
    in_specs = (P("orb", "dom", None, None), P("dom", None, None), P("orb", None), P(), P())
    out_specs = (P(None, "dom", None, None), P("orb", "dom", None, None))
    return jax.shard_map(
        per_device, mesh=mesh, in_specs=in_specs, out_specs=out_specs, check_vma=False
    )
```

```python
import functools

import jax
import jax.numpy as jnp
from jax import lax
from jax.experimental import pallas as pl
from jax.experimental.pallas import tpu as pltpu
from jax.sharding import PartitionSpec as P

CENTER = -5369.0 / 1800.0
SIDES = (12.0 / 7.0, -15.0 / 56.0, 10.0 / 189.0, -1.0 / 112.0, 2.0 / 1925.0, -1.0 / 16632.0)

MESH = pl.DeviceIdType.MESH
NB = 16
NX, NY, NZ = 8, 16, 128
NDOM, NORB, NCHIP = 16, 16, 8
HALO = 6
BF = jnp.bfloat16
F32 = jnp.float32


def split(value):
    high = value.astype(BF)
    return high, (value - high.astype(F32)).astype(BF)


def dot_nt(a, b):
    return lax.dot_general(a, b, (((1,), (1,)), ((), ())), preferred_element_type=F32)


def dot_nn(a, b):
    return lax.dot_general(a, b, (((1,), (0,)), ((), ())), preferred_element_type=F32)


def indicator(shape, row_of, col_of):
    rows = lax.broadcasted_iota(jnp.int32, shape, 0)
    cols = lax.broadcasted_iota(jnp.int32, shape, 1)
    return row_of(rows) == col_of(cols)


def kernel(
    block_ref, owner_ref, x_hbm, pot_hbm, rot_hbm, grad, w_ref, upd,
    x2, xh, xl, pot, rot, mask, remo, act, amat, pbuf, packed, panels,
    a1, a2, d1, b2, sb, send, recv, loc,
):
    dom = lax.axis_index("dom")
    orb = lax.axis_index("orb")
    z = lax.div(orb, 2)
    q = lax.rem(orb, 2)

    def chip(k):
        return lax.rem(z + (k + 2 * NCHIP), NCHIP)

    def peer(k):
        return (dom, 2 * chip(k) + q)

    def side(k):
        return (lax.rem(dom + (k + NDOM), NDOM), orb)

    sibling = (dom, orb + 1 - 2 * q)
    sems = iter(range(send.shape[0]))
    started = []

    def remote(src, dst, device):
        i = next(sems)
        copy = pltpu.make_async_remote_copy(
            src_ref=src, dst_ref=dst, send_sem=send.at[i], recv_sem=recv.at[i],
            device_id=device, device_id_type=MESH,
        )
        copy.start()
        started.append(copy)
        return copy

    def arrive(copies):
        for copy in copies:
            copy.wait_recv()

    loads = [
        pltpu.make_async_copy(src, dst, loc.at[i])
        for i, (src, dst) in enumerate(((x_hbm, x2.at[q]), (pot_hbm, pot), (rot_hbm, rot)))
    ]
    loads[0].start()
    barrier = pltpu.get_barrier_semaphore()
    for k in (8, 9, 7, 10, 6, 11, 5, 12, 4, 13, 3, 14, 2, 15, 1):
        pl.semaphore_signal(
            barrier, inc=1, device_id=(dom, lax.rem(orb + k, NORB)), device_id_type=MESH
        )
    for k in range(1, NDOM):
        pl.semaphore_signal(barrier, inc=1, device_id=side(k), device_id_type=MESH)
    for copy in loads[1:]:
        copy.start()
    for copy in loads:
        copy.wait()
    pl.semaphore_wait(barrier, NDOM + NORB - 2)

    def scatter_far(part, slot, h):
        whole, front, back = pl.ds(4 * h, 4), pl.ds(4 * h, 2), pl.ds(4 * h + 2, 2)
        return (
            remote(part(4).at[front], a2.at[slot, 0, front], peer(2)),
            remote(part(4).at[back], a2.at[slot, 1, back], peer(-2)),
            remote(part(3).at[whole], a1.at[slot, 0, whole], peer(1)),
            remote(part(-3).at[whole], a1.at[slot, 1, whole], peer(-1)),
        )

    def scatter_mid(part, slot, h, far):
        whole, front, back = pl.ds(4 * h, 4), pl.ds(4 * h, 2), pl.ds(4 * h + 2, 2)
        sent = []
        for i, sign, quarter in ((0, 1, front), (1, -1, back)):
            arrive((far[i], far[2 + i]))
            sb[slot, i, whole] = part(2 * sign)[whole] + a1[slot, i, whole]
            sb[slot, i, quarter] = sb[slot, i, quarter] + a2[slot, i, quarter]
            sent.append(remote(sb.at[slot, i, whole], b2.at[slot, i, whole], peer(2 * sign)))
        return tuple(sent)

    def scatter_near(part, slot, h):
        whole = pl.ds(4 * h, 4)
        return (
            remote(part(1).at[whole], d1.at[slot, 0, whole], peer(1)),
            remote(part(-1).at[whole], d1.at[slot, 1, whole], peer(-1)),
        )

    def scatter_sum(part, slot, h, copies):
        whole = pl.ds(4 * h, 4)
        arrive(copies)
        return (
            part(0)[whole]
            + (d1[slot, 0, whole] + d1[slot, 1, whole])
            + (b2[slot, 0, whole] + b2[slot, 1, whole])
        )

    def give(shard, k, to, planes):
        ref = shard(k).at[planes]
        return remote(ref, ref, peer(to))

    def gather_two(shard, h):
        whole = pl.ds(4 * h, 4)
        return give(shard, 0, 2, whole), give(shard, 0, -2, whole)

    def gather_one(shard, h):
        whole = pl.ds(4 * h, 4)
        return give(shard, 0, 1, whole), give(shard, 0, -1, whole)

    def gather_on(shard, h, two, arrived=lambda k, h: None):
        whole, front, back = pl.ds(4 * h, 4), pl.ds(4 * h, 2), pl.ds(4 * h + 2, 2)
        arrive(two[:1])
        ahead = give(shard, -2, 2, front), give(shard, -2, 1, whole)
        arrived(-2, h)
        arrive(two[1:])
        behind = give(shard, 2, -2, back), give(shard, 2, -1, whole)
        arrived(2, h)
        return ahead + behind

    order = (4, 3, -3, 2, -2, 1, -1, 0)

    def to_twin(k, parity):
        ref = x2.at[q, 2 * chip(k) + parity]
        return remote(ref, ref, sibling)

    wanted = [to_twin(k, 1 - q) for k in order]

    block = block_ref[0]
    root_core = lax.rem(block, 2)
    is_root = lax.div(block, 2) == z

    def masked(k):
        return mask.at[chip(k)]

    def fill(pairs):
        for k, copy in pairs:
            copy.wait_recv()
            i = 2 * chip(k) + q
            mine = jnp.where(root_core == 0, x2[0, i], x2[1, i])
            mask[chip(k)] = jnp.where(is_root, mine, 0.0)

    pairs = list(zip(order, wanted))
    fill(pairs[:3])
    far = [scatter_far(masked, 0, h) for h in range(2)]
    fill(pairs[3:])
    near = [scatter_near(masked, 0, h) for h in range(2)]
    others = [to_twin(k, q) for k in order]
    mid = [scatter_mid(masked, 0, h, far[h]) for h in range(2)]

    halo = []

    def lend(first, planes, to, shift):
        halo.append(remote(act.at[pl.ds(first, planes)], act.at[pl.ds(first + shift, planes)], side(to)))

    act[pl.ds(HALO, 4)] = scatter_sum(masked, 0, 0, near[0] + mid[0])
    lend(HALO, 4, -1, NX)
    lend(HALO + 2, 2, 1, -NX)
    act[pl.ds(HALO + 4, 4)] = scatter_sum(masked, 0, 1, near[1] + mid[1])
    lend(HALO + 4, 2, -1, NX)
    lend(HALO + 4, 4, 1, -NX)

    r_high, r_low = split(rot[...])
    r_both = jnp.concatenate([r_high, r_low], 0)
    for j in range(0, NORB, 2):
        base = (j // 8) * 128
        shape = (128, 256)
        pick = indicator(
            shape, lambda r: r + base, lambda c: (j + (c >> 7)) * NB + (c & (NB - 1))
        )
        both = dot_nn(r_both[:, base : base + 128], jnp.where(pick, 1.0, 0.0).astype(BF))
        both = both[:NB] + both[NB:]
        own = indicator((NB, 256), lambda r: r & 7, lambda c: (c & 127) >> 4)
        both = jnp.where(own, both, 0.0).reshape(2, 8, 256).sum(1)
        packed[j] = both[:, :128]
        packed[j + 1] = both[:, 128:]
    panels[orb] = packed[orb]
    panel_copies = []
    for k in range(1, NORB):
        to = lax.rem(orb + k, NORB)
        panel_copies.append(remote(packed.at[to], panels.at[orb], (dom, to)))

    field = act[pl.ds(HALO, NX)]
    inner = (pot[...] - 1.5 * CENTER) * field
    for k in range(1, 7):
        near = (
            pltpu.roll(field, k, 1) + pltpu.roll(field, NY - k, 1)
            + pltpu.roll(field, k, 2) + pltpu.roll(field, NZ - k, 2)
        )
        inner = inner - (0.5 * SIDES[k - 1]) * near
    arrive(others)
    for j in range(2):
        def cast(a, carry, j=j):
            high, low = split(x2[j, a])
            xh[j, a] = high
            xl[j, a] = low
            return carry
        lax.fori_loop(0, NB, cast, 0)
    arrive(halo)
    for k in range(1, 7):
        inner = inner - (0.5 * SIDES[k - 1]) * (act[pl.ds(HALO + k, NX)] + act[pl.ds(HALO - k, NX)])
    amat[z] = inner

    cols = 2 * NB * NY

    def shard(k):
        return amat.at[chip(k)]

    def same_y(rows):
        return indicator((rows, cols), lambda r: r & (NY - 1), lambda c: c & (NY - 1))

    def x_pairs():
        for x in range(0, NX, 2):
            yield x, *(
                jnp.concatenate([r[:, :, x].reshape(cols, NZ), r[:, :, x + 1].reshape(cols, NZ)], 1)
                for r in (xh, xl)
            )

    def project(batch, ks):
        rows = len(ks) * NY
        gram = jnp.zeros((rows, cols), F32)
        for x, h_pair, l_pair in x_pairs():
            a_pair = jnp.concatenate([
                jnp.concatenate([shard(k)[x] for k in ks], 0),
                jnp.concatenate([shard(k)[x + 1] for k in ks], 0),
            ], 1)
            a_high, a_low = split(a_pair)
            both = dot_nt(jnp.concatenate([a_high, a_low], 0), h_pair)
            gram = gram + (both[:rows] + both[rows:] + dot_nt(a_high, l_pair))
        summed = jnp.where(same_y(rows), gram, 0.0).reshape(len(ks), NY, cols).sum(1)
        summed = jnp.concatenate([summed, jnp.zeros((4 - len(ks), cols), F32)], 0)
        of_orbital = indicator((cols, 128), lambda r: r >> 4, lambda c: c)
        s_both = jnp.concatenate(split(summed), 0)
        summed = dot_nn(s_both, jnp.where(of_orbital, 1.0, 0.0).astype(BF))
        pbuf[batch, dom] = summed[:4] + summed[4:]
        ref = pbuf.at[batch, dom]
        return [remote(ref, ref, side(k)) for k in range(1, NDOM)]

    def remove(batch, ks, copies, halves):
        rows = len(ks) * NY
        arrive(copies)
        proj = pbuf[batch].sum(0) * (1.0 / (NX * NDOM * NY * NZ))
        to_rows = indicator((128, cols), lambda r: r, lambda c: c >> 4)
        spread = dot_nn(
            jnp.concatenate(split(proj), 0), jnp.where(to_rows, 1.0, 0.0).astype(BF)
        )
        keep = same_y(rows)
        weights = []
        for first in (0, 4):
            one = spread[first : first + len(ks)]
            one = jnp.broadcast_to(one[:, None, :], (len(ks), NY, cols)).reshape(rows, cols)
            weights.append(jnp.where(keep, one, 0.0).astype(BF))
        k_both = jnp.concatenate(weights, 0)
        for x, h_pair, l_pair in x_pairs():
            both = dot_nn(k_both, h_pair)
            part = both[:rows] + both[rows:] + dot_nn(weights[0], l_pair)
            for i, k in enumerate(ks):
                remo[chip(k), x] = part[i * NY : (i + 1) * NY, :NZ]
                remo[chip(k), x + 1] = part[i * NY : (i + 1) * NY, NZ:]
            if x == 2 or x == 6:
                halves(x // 4)

    one = [gather_one(shard, 0), gather_one(shard, 1)]
    two = [gather_two(shard, 0), gather_two(shard, 1)]
    arrive(one[0] + one[1])
    batches = ((0, 1, -1), (2, -2), (3, -3, 4))
    sums = [project(0, batches[0])]
    on = [gather_on(shard, 0, two[0])]
    on.append(gather_on(shard, 1, two[1]))
    sums.append(project(1, batches[1]))

    def removed(k):
        return remo.at[chip(k + 4)]

    def owned(k):
        return grad.at[2 * chip(k + 4) + q]

    far, mid, near, twins = [], [], [], [[], []]
    remove(0, batches[0], sums[0], lambda h: far.append(scatter_far(removed, 1, h)))
    arrive(on[0] + on[1])
    sums.append(project(2, batches[2]))
    remove(1, batches[1], sums[1], lambda h: None)
    mid.append(scatter_mid(removed, 1, 0, far[0]))
    mid.append(scatter_mid(removed, 1, 1, far[1]))
    remove(2, batches[2], sums[2], lambda h: near.append(scatter_near(removed, 1, h)))

    def to_sibling(k, h):
        ref = owned(k).at[pl.ds(4 * h, 4)]
        twins[h].append(remote(ref, ref, sibling))

    two, one, on = [], [], []
    for h in range(2):
        half = pl.ds(4 * h, 4)
        owned(0)[half] = amat[chip(4), half] - scatter_sum(removed, 1, h, near[h] + mid[h])
        two.append(gather_two(owned, h))
        one.append(gather_one(owned, h))
        to_sibling(0, h)

    arrive(panel_copies)
    rows = NB * NY
    panel = panels[owner_ref[0]]
    panel = jnp.broadcast_to(panel[:, None, :], (2, 8, 128)).reshape(NB, 128)
    own = indicator((NB, 128), lambda r: r & 7, lambda c: c >> 4)
    p_both = jnp.concatenate(split(jnp.where(own, panel, 0.0)), 0)
    of_column = indicator((rows, 128), lambda r: r >> 4, lambda c: c & (NB - 1))
    by_row = dot_nt(jnp.where(of_column, 1.0, 0.0).astype(BF), p_both).astype(BF)
    to_rows = indicator((NB, rows), lambda r: r, lambda c: c >> 4)
    to_rows = jnp.where(to_rows, 1.0, 0.0).astype(BF)
    keep = indicator((rows, rows), lambda r: r & (NY - 1), lambda c: c & (NY - 1))
    w_high, w_low = (
        jnp.where(keep, dot_nn(one_of, to_rows), 0.0).astype(BF)
        for one_of in (by_row[:, :NB], by_row[:, NB:])
    )
    w_both = jnp.concatenate([w_high, w_low], 0)

    w_ref[...] = w_both
    upd[:, 4:] = x2[q, :, 4:]

    for h in range(2):
        on.append(gather_on(owned, h, two[h], to_sibling))
    for h in range(2):
        for i, k in ((0, -1), (1, 1)):
            arrive(one[h][i : i + 1])
            to_sibling(k, h)
    for h in range(2):
        arrive(on[h][1:2])
        to_sibling(-3, h)
        arrive(on[h][3:4])
        to_sibling(3, h)
        arrive((on[h][0], on[h][2]))
        to_sibling(4, h)

    arrive(twins[0])
    for x in range(0, 4, 2):
        update(grad, w_both, x2.at[q], upd, x, x)
    arrive(twins[1])
    for copy in started:
        copy.wait_send()


def update(grad, w_both, old, new, x, at):
    rows = NB * NY
    g_pair = jnp.concatenate([grad[:, x].reshape(rows, NZ), grad[:, x + 1].reshape(rows, NZ)], 1)
    g_high, g_low = split(g_pair)
    both = dot_nn(w_both, g_high)
    part = both[:rows] + both[rows:] + dot_nn(w_both[:rows], g_low)
    new[:, at] = old[:, x] + part[:, :NZ].reshape(NB, NY, NZ)
    new[:, at + 1] = old[:, x + 1] + part[:, NZ:].reshape(NB, NY, NZ)


def update_kernel(grad, w_ref, upd, grad_hbm, upd_hbm, done, sem):
    outs = []

    def out(src, dst):
        outs.append(pltpu.make_async_copy(src, dst, sem.at[len(outs)]))
        outs[-1].start()

    out(upd.at[:, pl.ds(0, 4)], upd_hbm.at[:, pl.ds(0, 4)])
    out(grad, grad_hbm)
    w_both = w_ref[...]
    for x in range(4, NX, 2):
        pair = pl.ds(x, 2)
        update(grad, w_both, upd, done, x, x - 4)
        out(done.at[:, pl.ds(x - 4, 2)], upd_hbm.at[:, pair])
    for copy in outs:
        copy.wait()


def per_device(orbitals, potential, rotation, block, owner):
    shard = (NX, NY, NZ)
    scratch = [
        pltpu.VMEM((2, NB, *shard), F32),
        pltpu.VMEM((2, NB, *shard), BF),
        pltpu.VMEM((2, NB, *shard), BF),
        pltpu.VMEM(shard, F32),
        pltpu.VMEM((NB, NB * NORB), F32),
        pltpu.VMEM((NCHIP, *shard), F32),
        pltpu.VMEM((NCHIP, *shard), F32),
        pltpu.VMEM((NX + 2 * HALO, NY, NZ), F32),
        pltpu.VMEM((NCHIP, *shard), F32),
        pltpu.VMEM((3, NDOM, 4, 128), F32),
        pltpu.VMEM((NORB, 2, 128), F32),
        pltpu.VMEM((NORB, 2, 128), F32),
        pltpu.VMEM((2, 2, *shard), F32),
        pltpu.VMEM((2, 2, *shard), F32),
        pltpu.VMEM((2, 2, *shard), F32),
        pltpu.VMEM((2, 2, *shard), F32),
        pltpu.VMEM((2, 2, *shard), F32),
        pltpu.SemaphoreType.DMA((160,)),
        pltpu.SemaphoreType.DMA((160,)),
        pltpu.SemaphoreType.DMA((8,)),
    ]
    hbm = pl.BlockSpec(memory_space=pl.ANY)
    smem = pl.BlockSpec(memory_space=pltpu.SMEM)
    vmem = pl.BlockSpec(memory_space=pltpu.VMEM)
    whole = jax.ShapeDtypeStruct((NB, *shard), F32)
    arrays = (pltpu.with_memory_space_constraint(v, pltpu.HBM) for v in (orbitals, potential, rotation))
    gradient, weights, updated = pl.pallas_call(
        kernel,
        out_shape=(whole, jax.ShapeDtypeStruct((2 * NB * NY, NB * NY), BF), whole),
        in_specs=[smem, smem, hbm, hbm, hbm],
        out_specs=(vmem, vmem, vmem),
        scratch_shapes=scratch,
        compiler_params=pltpu.CompilerParams(
            collective_id=0, has_side_effects=True, vmem_limit_bytes=40 << 20
        ),
        cost_estimate=pl.CostEstimate(flops=1 << 28, bytes_accessed=3 << 20, transcendentals=0),
        name="gradient",
    )(block, owner, *arrays)
    return pl.pallas_call(
        update_kernel,
        out_shape=(whole, whole),
        in_specs=[vmem, vmem, vmem],
        out_specs=(hbm, hbm),
        scratch_shapes=[
            pltpu.VMEM((NB, NX // 2, NY, NZ), F32),
            pltpu.SemaphoreType.DMA((4,)),
        ],
        compiler_params=pltpu.CompilerParams(vmem_limit_bytes=16 << 20),
        cost_estimate=pl.CostEstimate(flops=1 << 28, bytes_accessed=4 << 20, transcendentals=0),
        name="update",
    )(gradient, weights, updated)


def solution(mesh):
    in_specs = (P("orb", "dom", None, None), P("dom", None, None), P("orb", None), P(), P())
    out_specs = (P(None, "dom", None, None), P("orb", "dom", None, None))
    return jax.shard_map(
        per_device, mesh=mesh, in_specs=in_specs, out_specs=out_specs, check_vma=False
    )
```

```python
import itertools
import math

import jax
import jax.numpy as jnp
from jax import lax
from jax.experimental import pallas as pl
from jax.experimental.pallas import tpu as pltpu
from jax.sharding import PartitionSpec as P

CENTER = -5369.0 / 1800.0
SIDES = (12.0 / 7.0, -15.0 / 56.0, 10.0 / 189.0, -1.0 / 112.0, 2.0 / 1925.0, -1.0 / 16632.0)

MESH = pl.DeviceIdType.MESH
NB = 16
NX, NY, NZ = 8, 16, 128
NDOM, NORB, NCHIP = 16, 16, 8
HALO = 6
BF = jnp.bfloat16
F32 = jnp.float32


def split(value):
    high = value.astype(BF)
    return high, (value - high.astype(F32)).astype(BF)


def dot_nt(a, b):
    return lax.dot_general(a, b, (((1,), (1,)), ((), ())), preferred_element_type=F32)


def dot_nn(a, b):
    return lax.dot_general(a, b, (((1,), (0,)), ((), ())), preferred_element_type=F32)


def indicator(shape, row_of, col_of):
    rows = lax.broadcasted_iota(jnp.int32, shape, 0)
    cols = lax.broadcasted_iota(jnp.int32, shape, 1)
    return row_of(rows) == col_of(cols)


def kernel(
    block_ref, owner_ref, x_hbm, pot_hbm, rot_hbm, grad, w_ref, upd,
    x2, xh, xl, pot, rot, mask, remo, act, amat, pbuf, packed, panels,
    a1, a2, d1, b2, sb, send, recv, loc,
):
    dom = lax.axis_index("dom")
    orb = lax.axis_index("orb")
    z = lax.div(orb, 2)
    q = lax.rem(orb, 2)

    def chip(k):
        return lax.rem(z + (k + 2 * NCHIP), NCHIP)

    def peer(k):
        return (dom, 2 * chip(k) + q)

    def side(k):
        return (lax.rem(dom + (k + NDOM), NDOM), orb)

    sibling = (dom, orb + 1 - 2 * q)
    groups = itertools.count()
    sent = [dict(sem=i, rows=0) for i in range(send.shape[0])]
    phase = [0]

    def new(span=None):
        return dict(sem=next(groups), rows=0, span=span)

    def remote(src, dst, device, group, sends=None):
        sends = sent[phase[0]] if sends is None else sends
        pltpu.make_async_remote_copy(
            src_ref=src, dst_ref=dst, send_sem=send.at[sends["sem"]], recv_sem=recv.at[group["sem"]],
            device_id=device, device_id_type=MESH,
        ).start()
        for one in (group, sends):
            one["rows"] += math.prod(src.shape[:-1])

    def span(group):
        planes = group["rows"] // NY
        if group.get("span") is not None:
            ref = group["span"]
        elif planes <= act.shape[0]:
            ref = act.at[pl.ds(0, planes)]
        else:
            ref = x2.at[0, pl.ds(0, planes // NX)]
        assert math.prod(ref.shape[:-1]) == group["rows"]
        return pltpu.make_async_remote_copy(
            src_ref=ref, dst_ref=ref, send_sem=send.at[group["sem"] % len(sent)],
            recv_sem=recv.at[group["sem"]], device_id=sibling, device_id_type=MESH,
        )

    def arrive(*waited):
        for group in waited:
            span(group).wait_recv()

    loads = [
        pltpu.make_async_copy(src, dst, loc.at[i])
        for i, (src, dst) in enumerate(((x_hbm, x2.at[q]), (pot_hbm, pot), (rot_hbm, rot)))
    ]
    loads[0].start()
    barrier = pltpu.get_barrier_semaphore()
    for k in (8, 9, 7, 10, 6, 11, 5, 12, 4, 13, 3, 14, 2, 15, 1):
        pl.semaphore_signal(
            barrier, inc=1, device_id=(dom, lax.rem(orb + k, NORB)), device_id_type=MESH
        )
    for k in range(1, NDOM):
        pl.semaphore_signal(barrier, inc=1, device_id=side(k), device_id_type=MESH)
    for copy in loads[1:]:
        copy.start()
    for copy in loads:
        copy.wait()
    pl.semaphore_wait(barrier, NDOM + NORB - 2)

    def scatter_far(part, slot, h):
        whole, front, back = pl.ds(4 * h, 4), pl.ds(4 * h, 2), pl.ds(4 * h + 2, 2)
        up, down = new(), new()
        remote(part(4).at[front], a2.at[slot, 0, front], peer(2), up)
        remote(part(4).at[back], a2.at[slot, 1, back], peer(-2), down)
        remote(part(3).at[whole], a1.at[slot, 0, whole], peer(1), up)
        remote(part(-3).at[whole], a1.at[slot, 1, whole], peer(-1), down)
        return up, down

    def scatter_mid(part, slot, h, far, last):
        whole, front, back = pl.ds(4 * h, 4), pl.ds(4 * h, 2), pl.ds(4 * h + 2, 2)
        for i, sign, quarter in ((0, 1, front), (1, -1, back)):
            arrive(far[i])
            sb[slot, i, whole] = part(2 * sign)[whole] + a1[slot, i, whole]
            sb[slot, i, quarter] = sb[slot, i, quarter] + a2[slot, i, quarter]
            remote(sb.at[slot, i, whole], b2.at[slot, i, whole], peer(2 * sign), last)

    def scatter_near(part, slot, h, last):
        whole = pl.ds(4 * h, 4)
        remote(part(1).at[whole], d1.at[slot, 0, whole], peer(1), last)
        remote(part(-1).at[whole], d1.at[slot, 1, whole], peer(-1), last)

    def scatter_sum(part, slot, h, last):
        whole = pl.ds(4 * h, 4)
        arrive(last)
        return (
            part(0)[whole]
            + (d1[slot, 0, whole] + d1[slot, 1, whole])
            + (b2[slot, 0, whole] + b2[slot, 1, whole])
        )

    def give(shard, k, to, planes, group):
        ref = shard(k).at[planes]
        remote(ref, ref, peer(to), group)

    def gather_two(shard, h):
        whole = pl.ds(4 * h, 4)
        two = new(), new()
        give(shard, 0, 2, whole, two[0])
        give(shard, 0, -2, whole, two[1])
        return two

    def gather_one(shard, h, group):
        whole = pl.ds(4 * h, 4)
        give(shard, 0, 1, whole, group)
        give(shard, 0, -1, whole, group)

    def gather_on(shard, h, two, three, four, arrived=lambda k, h: None):
        whole, front, back = pl.ds(4 * h, 4), pl.ds(4 * h, 2), pl.ds(4 * h + 2, 2)
        arrive(two[0])
        give(shard, -2, 2, front, four)
        give(shard, -2, 1, whole, three)
        arrived(-2, h)
        arrive(two[1])
        give(shard, 2, -2, back, four)
        give(shard, 2, -1, whole, three)
        arrived(2, h)

    order = (4, 3, -3, 2, -2, 1, -1, 0)

    def to_twin(ks, parity):
        group = new()
        for k in ks:
            ref = x2.at[q, 2 * chip(k) + parity]
            remote(ref, ref, sibling, group)
        return group

    wanted = to_twin(order[:3], 1 - q), to_twin(order[3:], 1 - q)

    block = block_ref[0]
    root_core = lax.rem(block, 2)
    is_root = lax.div(block, 2) == z

    def masked(k):
        return mask.at[chip(k)]

    def fill(ks, copies):
        arrive(copies)
        for k in ks:
            i = 2 * chip(k) + q
            mine = jnp.where(root_core == 0, x2[0, i], x2[1, i])
            mask[chip(k)] = jnp.where(is_root, mine, 0.0)

    fill(order[:3], wanted[0])
    phase[0] = 1
    far = [scatter_far(masked, 0, h) for h in range(2)]
    fill(order[3:], wanted[1])
    last = [new(), new()]
    for h in range(2):
        scatter_near(masked, 0, h, last[h])
    others = to_twin(order, q)
    for h in range(2):
        scatter_mid(masked, 0, h, far[h], last[h])

    phase[0] = 2
    halo = new()

    def lend(first, planes, to, shift):
        src, dst = act.at[pl.ds(first, planes)], act.at[pl.ds(first + shift, planes)]
        remote(src, dst, side(to), halo)

    act[pl.ds(HALO, 4)] = scatter_sum(masked, 0, 0, last[0])
    lend(HALO, 4, -1, NX)
    lend(HALO + 2, 2, 1, -NX)
    act[pl.ds(HALO + 4, 4)] = scatter_sum(masked, 0, 1, last[1])
    lend(HALO + 4, 2, -1, NX)
    lend(HALO + 4, 4, 1, -NX)

    r_high, r_low = split(rot[...])
    r_both = jnp.concatenate([r_high, r_low], 0)
    for j in range(0, NORB, 2):
        base = (j // 8) * 128
        shape = (128, 256)
        pick = indicator(
            shape, lambda r: r + base, lambda c: (j + (c >> 7)) * NB + (c & (NB - 1))
        )
        both = dot_nn(r_both[:, base : base + 128], jnp.where(pick, 1.0, 0.0).astype(BF))
        both = both[:NB] + both[NB:]
        own = indicator((NB, 256), lambda r: r & 7, lambda c: (c & 127) >> 4)
        both = jnp.where(own, both, 0.0).reshape(2, 8, 256).sum(1)
        packed[j] = both[:, :128]
        packed[j + 1] = both[:, 128:]
    panels[orb] = packed[orb]
    panel_copies = new(panels.at[pl.ds(0, NORB - 1)])
    sent[6]["span"] = panel_copies["span"]
    for k in range(1, NORB):
        to = lax.rem(orb + k, NORB)
        remote(packed.at[to], panels.at[orb], (dom, to), panel_copies, sent[6])

    field = act[pl.ds(HALO, NX)]
    inner = (pot[...] - 1.5 * CENTER) * field
    for k in range(1, 7):
        near = (
            pltpu.roll(field, k, 1) + pltpu.roll(field, NY - k, 1)
            + pltpu.roll(field, k, 2) + pltpu.roll(field, NZ - k, 2)
        )
        inner = inner - (0.5 * SIDES[k - 1]) * near
    arrive(others)
    for j in range(2):
        def cast(a, carry, j=j):
            high, low = split(x2[j, a])
            xh[j, a] = high
            xl[j, a] = low
            return carry
        lax.fori_loop(0, NB, cast, 0)
    arrive(halo)
    for k in range(1, 7):
        inner = inner - (0.5 * SIDES[k - 1]) * (act[pl.ds(HALO + k, NX)] + act[pl.ds(HALO - k, NX)])
    amat[z] = inner

    cols = 2 * NB * NY

    def shard(k):
        return amat.at[chip(k)]

    def same_y(rows):
        return indicator((rows, cols), lambda r: r & (NY - 1), lambda c: c & (NY - 1))

    def x_pairs():
        for x in range(0, NX, 2):
            yield x, *(
                jnp.concatenate([r[:, :, x].reshape(cols, NZ), r[:, :, x + 1].reshape(cols, NZ)], 1)
                for r in (xh, xl)
            )

    def project(batch, ks):
        rows = len(ks) * NY
        gram = jnp.zeros((rows, cols), F32)
        for x, h_pair, l_pair in x_pairs():
            a_pair = jnp.concatenate([
                jnp.concatenate([shard(k)[x] for k in ks], 0),
                jnp.concatenate([shard(k)[x + 1] for k in ks], 0),
            ], 1)
            a_high, a_low = split(a_pair)
            both = dot_nt(jnp.concatenate([a_high, a_low], 0), h_pair)
            gram = gram + (both[:rows] + both[rows:] + dot_nt(a_high, l_pair))
        summed = jnp.where(same_y(rows), gram, 0.0).reshape(len(ks), NY, cols).sum(1)
        summed = jnp.concatenate([summed, jnp.zeros((4 - len(ks), cols), F32)], 0)
        of_orbital = indicator((cols, 128), lambda r: r >> 4, lambda c: c)
        s_both = jnp.concatenate(split(summed), 0)
        summed = dot_nn(s_both, jnp.where(of_orbital, 1.0, 0.0).astype(BF))
        pbuf[batch, dom] = summed[:4] + summed[4:]
        ref = pbuf.at[batch, dom]
        sums = new(pbuf.at[batch, pl.ds(0, NDOM - 1)])
        sent[7 + batch]["span"] = sums["span"]
        for k in range(1, NDOM):
            remote(ref, ref, side(k), sums, sent[7 + batch])
        return sums

    def remove(batch, ks, copies, halves):
        rows = len(ks) * NY
        arrive(copies)
        proj = pbuf[batch].sum(0) * (1.0 / (NX * NDOM * NY * NZ))
        to_rows = indicator((128, cols), lambda r: r, lambda c: c >> 4)
        spread = dot_nn(
            jnp.concatenate(split(proj), 0), jnp.where(to_rows, 1.0, 0.0).astype(BF)
        )
        keep = same_y(rows)
        weights = []
        for first in (0, 4):
            one = spread[first : first + len(ks)]
            one = jnp.broadcast_to(one[:, None, :], (len(ks), NY, cols)).reshape(rows, cols)
            weights.append(jnp.where(keep, one, 0.0).astype(BF))
        k_both = jnp.concatenate(weights, 0)
        for x, h_pair, l_pair in x_pairs():
            both = dot_nn(k_both, h_pair)
            part = both[:rows] + both[rows:] + dot_nn(weights[0], l_pair)
            for i, k in enumerate(ks):
                remo[chip(k), x] = part[i * NY : (i + 1) * NY, :NZ]
                remo[chip(k), x + 1] = part[i * NY : (i + 1) * NY, NZ:]
            if x == 2 or x == 6:
                halves(x // 4)

    phase[0] = 3
    one, on = new(), new()
    gather_one(shard, 0, one)
    gather_one(shard, 1, one)
    two = [gather_two(shard, 0), gather_two(shard, 1)]
    arrive(one)
    batches = ((0, 1, -1), (2, -2), (3, -3, 4))
    sums = [project(0, batches[0])]
    gather_on(shard, 0, two[0], on, on)
    gather_on(shard, 1, two[1], on, on)
    sums.append(project(1, batches[1]))

    def removed(k):
        return remo.at[chip(k + 4)]

    def owned(k):
        return grad.at[2 * chip(k + 4) + q]

    phase[0] = 4
    far, last, twins = [], [new(), new()], [new(), new()]
    remove(0, batches[0], sums[0], lambda h: far.append(scatter_far(removed, 1, h)))
    arrive(on)
    sums.append(project(2, batches[2]))
    remove(1, batches[1], sums[1], lambda h: None)
    for h in range(2):
        scatter_mid(removed, 1, h, far[h], last[h])
    remove(2, batches[2], sums[2], lambda h: scatter_near(removed, 1, h, last[h]))

    phase[0] = 5

    def to_sibling(k, h):
        ref = owned(k).at[pl.ds(4 * h, 4)]
        remote(ref, ref, sibling, twins[h])

    two, one, three, four = [], [new(), new()], [new(), new()], [new(), new()]
    for h in range(2):
        half = pl.ds(4 * h, 4)
        owned(0)[half] = amat[chip(4), half] - scatter_sum(removed, 1, h, last[h])
        two.append(gather_two(owned, h))
        gather_one(owned, h, one[h])
        to_sibling(0, h)

    arrive(panel_copies)
    rows = NB * NY
    panel = panels[owner_ref[0]]
    panel = jnp.broadcast_to(panel[:, None, :], (2, 8, 128)).reshape(NB, 128)
    own = indicator((NB, 128), lambda r: r & 7, lambda c: c >> 4)
    p_both = jnp.concatenate(split(jnp.where(own, panel, 0.0)), 0)
    of_column = indicator((rows, 128), lambda r: r >> 4, lambda c: c & (NB - 1))
    by_row = dot_nt(jnp.where(of_column, 1.0, 0.0).astype(BF), p_both).astype(BF)
    to_rows = indicator((NB, rows), lambda r: r, lambda c: c >> 4)
    to_rows = jnp.where(to_rows, 1.0, 0.0).astype(BF)
    keep = indicator((rows, rows), lambda r: r & (NY - 1), lambda c: c & (NY - 1))
    w_high, w_low = (
        jnp.where(keep, dot_nn(one_of, to_rows), 0.0).astype(BF)
        for one_of in (by_row[:, :NB], by_row[:, NB:])
    )
    w_both = jnp.concatenate([w_high, w_low], 0)

    w_ref[...] = w_both
    upd[:, 4:] = x2[q, :, 4:]

    for h in range(2):
        gather_on(owned, h, two[h], three[h], four[h], to_sibling)
    for h in range(2):
        arrive(one[h])
        to_sibling(-1, h)
        to_sibling(1, h)
    for h in range(2):
        arrive(three[h])
        to_sibling(-3, h)
        to_sibling(3, h)
        arrive(four[h])
        to_sibling(4, h)

    arrive(twins[0])
    for x in range(0, 4, 2):
        update(grad, w_both, x2.at[q], upd, x, x)
    arrive(twins[1])
    for group in sent:
        span(group).wait_send()
    assert next(groups) == recv.shape[0]


def update(grad, w_both, old, new, x, at):
    rows = NB * NY
    g_pair = jnp.concatenate([grad[:, x].reshape(rows, NZ), grad[:, x + 1].reshape(rows, NZ)], 1)
    g_high, g_low = split(g_pair)
    both = dot_nn(w_both, g_high)
    part = both[:rows] + both[rows:] + dot_nn(w_both[:rows], g_low)
    new[:, at] = old[:, x] + part[:, :NZ].reshape(NB, NY, NZ)
    new[:, at + 1] = old[:, x + 1] + part[:, NZ:].reshape(NB, NY, NZ)


def update_kernel(grad, w_ref, upd, grad_hbm, upd_hbm, done, sem):
    outs = []

    def out(src, dst):
        outs.append(pltpu.make_async_copy(src, dst, sem.at[len(outs)]))
        outs[-1].start()

    out(upd.at[:, pl.ds(0, 4)], upd_hbm.at[:, pl.ds(0, 4)])
    out(grad, grad_hbm)
    w_both = w_ref[...]
    for x in range(4, NX, 2):
        pair = pl.ds(x, 2)
        update(grad, w_both, upd, done, x, x - 4)
        out(done.at[:, pl.ds(x - 4, 2)], upd_hbm.at[:, pair])
    for copy in outs:
        copy.wait()


def per_device(orbitals, potential, rotation, block, owner):
    shard = (NX, NY, NZ)
    scratch = [
        pltpu.VMEM((2, NB, *shard), F32),
        pltpu.VMEM((2, NB, *shard), BF),
        pltpu.VMEM((2, NB, *shard), BF),
        pltpu.VMEM(shard, F32),
        pltpu.VMEM((NB, NB * NORB), F32),
        pltpu.VMEM((NCHIP, *shard), F32),
        pltpu.VMEM((NCHIP, *shard), F32),
        pltpu.VMEM((NX + 2 * HALO, NY, NZ), F32),
        pltpu.VMEM((NCHIP, *shard), F32),
        pltpu.VMEM((3, NDOM, 4, 128), F32),
        pltpu.VMEM((NORB, 2, 128), F32),
        pltpu.VMEM((NORB, 2, 128), F32),
        pltpu.VMEM((2, 2, *shard), F32),
        pltpu.VMEM((2, 2, *shard), F32),
        pltpu.VMEM((2, 2, *shard), F32),
        pltpu.VMEM((2, 2, *shard), F32),
        pltpu.VMEM((2, 2, *shard), F32),
        pltpu.SemaphoreType.DMA((10,)),
        pltpu.SemaphoreType.DMA((38,)),
        pltpu.SemaphoreType.DMA((3,)),
    ]
    hbm = pl.BlockSpec(memory_space=pl.ANY)
    smem = pl.BlockSpec(memory_space=pltpu.SMEM)
    vmem = pl.BlockSpec(memory_space=pltpu.VMEM)
    whole = jax.ShapeDtypeStruct((NB, *shard), F32)
    arrays = (pltpu.with_memory_space_constraint(v, pltpu.HBM) for v in (orbitals, potential, rotation))
    gradient, weights, updated = pl.pallas_call(
        kernel,
        out_shape=(whole, jax.ShapeDtypeStruct((2 * NB * NY, NB * NY), BF), whole),
        in_specs=[smem, smem, hbm, hbm, hbm],
        out_specs=(vmem, vmem, vmem),
        scratch_shapes=scratch,
        compiler_params=pltpu.CompilerParams(
            collective_id=0, has_side_effects=True, vmem_limit_bytes=40 << 20
        ),
        cost_estimate=pl.CostEstimate(flops=1 << 28, bytes_accessed=3 << 20, transcendentals=0),
        name="gradient",
    )(block, owner, *arrays)
    return pl.pallas_call(
        update_kernel,
        out_shape=(whole, whole),
        in_specs=[vmem, vmem, vmem],
        out_specs=(hbm, hbm),
        scratch_shapes=[
            pltpu.VMEM((NB, NX // 2, NY, NZ), F32),
            pltpu.SemaphoreType.DMA((4,)),
        ],
        compiler_params=pltpu.CompilerParams(vmem_limit_bytes=16 << 20),
        cost_estimate=pl.CostEstimate(flops=1 << 28, bytes_accessed=4 << 20, transcendentals=0),
        name="update",
    )(gradient, weights, updated)


def solution(mesh):
    in_specs = (P("orb", "dom", None, None), P("dom", None, None), P("orb", None), P(), P())
    out_specs = (P(None, "dom", None, None), P("orb", "dom", None, None))
    return jax.shard_map(
        per_device, mesh=mesh, in_specs=in_specs, out_specs=out_specs, check_vma=False
    )
```

```python
import functools
import itertools
import math

import jax
import jax.numpy as jnp
from jax import lax
from jax.experimental import pallas as pl
from jax.experimental.pallas import tpu as pltpu
from jax.sharding import PartitionSpec as P

CENTER = -5369.0 / 1800.0
SIDES = (12.0 / 7.0, -15.0 / 56.0, 10.0 / 189.0, -1.0 / 112.0, 2.0 / 1925.0, -1.0 / 16632.0)

MESH = pl.DeviceIdType.MESH
NB = 16
NX, NY, NZ = 8, 16, 128
NDOM, NORB, NCHIP = 16, 16, 8
HALO = 6
BF = jnp.bfloat16
F32 = jnp.float32


def split(value):
    high = value.astype(BF)
    return high, (value - high.astype(F32)).astype(BF)


def dot_nt(a, b):
    return lax.dot_general(a, b, (((1,), (1,)), ((), ())), preferred_element_type=F32)


def dot_nn(a, b):
    return lax.dot_general(a, b, (((1,), (0,)), ((), ())), preferred_element_type=F32)


def indicator(shape, row_of, col_of):
    rows = lax.broadcasted_iota(jnp.int32, shape, 0)
    cols = lax.broadcasted_iota(jnp.int32, shape, 1)
    return row_of(rows) == col_of(cols)


def scatter_kernel(root, x_hbm, mine, sems):
    dom = lax.axis_index("dom")
    orb = lax.axis_index("orb")
    chip, core = root // 2, root % 2
    barrier = pltpu.get_barrier_semaphore()

    def send(c):
        return pltpu.make_async_remote_copy(
            src_ref=x_hbm.at[c], dst_ref=mine, send_sem=sems.at[0], recv_sem=sems.at[1],
            device_id=(dom, c), device_id_type=MESH,
        )

    @pl.when(orb == root)
    def _():
        pl.semaphore_wait(barrier, NORB - 1)
        for k in (4, 3, -3, 2, -2, 1, -1, 0):
            for c in (2 * ((chip + k) % NCHIP), 2 * ((chip + k) % NCHIP) + 1):
                if c != root:
                    send(c).start()
        own = pltpu.make_async_copy(x_hbm.at[root], mine, sems.at[2])
        own.start()
        own.wait()
        rest = x_hbm.at[pl.ds(0, NORB - 1)]
        pltpu.make_async_remote_copy(
            src_ref=rest, dst_ref=rest, send_sem=sems.at[0], recv_sem=sems.at[1],
            device_id=(dom, 2 * chip + 1 - core), device_id_type=MESH,
        ).wait_send()

    @pl.when(orb != root)
    def _():
        pl.semaphore_signal(barrier, inc=1, device_id=(dom, root), device_id_type=MESH)
        send(root).wait_recv()


def scattered(root, x_hbm):
    return pl.pallas_call(
        functools.partial(scatter_kernel, root),
        out_shape=jax.ShapeDtypeStruct((NX, NY, NZ), F32),
        in_specs=[pl.BlockSpec(memory_space=pl.ANY)],
        out_specs=pl.BlockSpec(memory_space=pltpu.VMEM),
        scratch_shapes=[pltpu.SemaphoreType.DMA((3,))],
        compiler_params=pltpu.CompilerParams(
            collective_id=root, has_side_effects=True, vmem_limit_bytes=40 << 20
        ),
        name="scatter",
    )(pltpu.with_memory_space_constraint(x_hbm, pltpu.HBM))


def kernel(
    owner_ref, mine, x_hbm, pot_hbm, rot_hbm, grad, w_ref, upd,
    x2, xh, xl, pot, rot, remo, act, amat, pbuf, packed, panels,
    a1, a2, d1, b2, sb, send, recv, loc, greetings,
):
    dom = lax.axis_index("dom")
    orb = lax.axis_index("orb")
    z = lax.div(orb, 2)
    q = lax.rem(orb, 2)

    def chip(k):
        return lax.rem(z + (k + 2 * NCHIP), NCHIP)

    def peer(k):
        return (dom, 2 * chip(k) + q)

    def side(k):
        return (lax.rem(dom + (k + NDOM), NDOM), orb)

    sibling = (dom, orb + 1 - 2 * q)
    groups = itertools.count()
    sent = [dict(sem=i, rows=0) for i in range(send.shape[0])]
    phase = [0]

    def new(span=None):
        return dict(sem=next(groups), rows=0, span=span)

    def remote(src, dst, device, group, sends=None):
        sends = sent[phase[0]] if sends is None else sends
        pltpu.make_async_remote_copy(
            src_ref=src, dst_ref=dst, send_sem=send.at[sends["sem"]], recv_sem=recv.at[group["sem"]],
            device_id=device, device_id_type=MESH,
        ).start()
        for one in (group, sends):
            one["rows"] += math.prod(src.shape[:-1])

    def span(group):
        planes = group["rows"] // NY
        if group.get("span") is not None:
            ref = group["span"]
        elif planes <= act.shape[0]:
            ref = act.at[pl.ds(0, planes)]
        else:
            ref = x2.at[0, pl.ds(0, planes // NX)]
        assert math.prod(ref.shape[:-1]) == group["rows"]
        return pltpu.make_async_remote_copy(
            src_ref=ref, dst_ref=ref, send_sem=send.at[group["sem"] % len(sent)],
            recv_sem=recv.at[group["sem"]], device_id=sibling, device_id_type=MESH,
        )

    def arrive(*waited):
        for group in waited:
            span(group).wait_recv()

    loads = [
        pltpu.make_async_copy(src, dst, loc.at[i])
        for i, (src, dst) in enumerate(((x_hbm, x2.at[q]), (pot_hbm, pot), (rot_hbm, rot)))
    ]
    loads[0].start()
    row, col = lax.div(dom, 4), lax.rem(dom, 4)
    around = [
        (4 * lax.rem(row + i, 4) + lax.rem(col + j, 4), orb) for i, j in ((0, 1), (0, 3), (1, 0), (3, 0))
    ]
    near = [peer(2), peer(-2), side(1), side(-1), *around, peer(1), peer(-1), sibling]
    barrier = pltpu.get_barrier_semaphore()
    for device in near:
        pl.semaphore_signal(barrier, inc=1, device_id=device, device_id_type=MESH)
    for copy in loads[1:]:
        copy.start()
    pl.semaphore_wait(barrier, len(near))

    def greet(i):
        if i > 0:
            pl.semaphore_wait(greetings.at[i - 1], len(around))
        if i < 3:
            for device in around:
                pl.semaphore_signal(greetings.at[i], inc=1, device_id=device, device_id_type=MESH)

    def scatter_far(part, slot, h):
        whole, front, back = pl.ds(4 * h, 4), pl.ds(4 * h, 2), pl.ds(4 * h + 2, 2)
        up, down = new(), new()
        remote(part(4).at[front], a2.at[slot, 0, front], peer(2), up)
        remote(part(4).at[back], a2.at[slot, 1, back], peer(-2), down)
        remote(part(3).at[whole], a1.at[slot, 0, whole], peer(1), up)
        remote(part(-3).at[whole], a1.at[slot, 1, whole], peer(-1), down)
        return up, down

    def scatter_mid(part, slot, h, far, last):
        whole, front, back = pl.ds(4 * h, 4), pl.ds(4 * h, 2), pl.ds(4 * h + 2, 2)
        for i, sign, quarter in ((0, 1, front), (1, -1, back)):
            arrive(far[i])
            sb[slot, i, whole] = part(2 * sign)[whole] + a1[slot, i, whole]
            sb[slot, i, quarter] = sb[slot, i, quarter] + a2[slot, i, quarter]
            remote(sb.at[slot, i, whole], b2.at[slot, i, whole], peer(2 * sign), last)

    def scatter_near(part, slot, h, last):
        whole = pl.ds(4 * h, 4)
        remote(part(1).at[whole], d1.at[slot, 0, whole], peer(1), last)
        remote(part(-1).at[whole], d1.at[slot, 1, whole], peer(-1), last)

    def scatter_sum(part, slot, h, last):
        whole = pl.ds(4 * h, 4)
        arrive(last)
        return (
            part(0)[whole]
            + (d1[slot, 0, whole] + d1[slot, 1, whole])
            + (b2[slot, 0, whole] + b2[slot, 1, whole])
        )

    def give(shard, k, to, planes, group):
        ref = shard(k).at[planes]
        remote(ref, ref, peer(to), group)

    def gather_two(shard, h):
        whole = pl.ds(4 * h, 4)
        two = new(), new()
        give(shard, 0, 2, whole, two[0])
        give(shard, 0, -2, whole, two[1])
        return two

    def gather_one(shard, h, group):
        whole = pl.ds(4 * h, 4)
        give(shard, 0, 1, whole, group)
        give(shard, 0, -1, whole, group)

    def gather_on(shard, h, two, three, four, arrived=lambda k, h: None):
        whole, front, back = pl.ds(4 * h, 4), pl.ds(4 * h, 2), pl.ds(4 * h + 2, 2)
        arrive(two[0])
        give(shard, -2, 2, front, four)
        give(shard, -2, 1, whole, three)
        arrived(-2, h)
        arrive(two[1])
        give(shard, 2, -2, back, four)
        give(shard, 2, -1, whole, three)
        arrived(2, h)

    phase[0] = 1
    halo = new()

    def lend(first, planes, to, shift):
        src, dst = mine.at[pl.ds(first, planes)], act.at[pl.ds(first + shift, planes)]
        remote(src, dst, side(to), halo)

    lend(0, HALO, -1, HALO + NX)
    lend(NX - HALO, HALO, 1, HALO - NX)
    greet(0)
    for copy in loads:
        copy.wait()
    phase[0] = 0
    others = new()
    remote(x2.at[q], x2.at[q], sibling, others)
    act[pl.ds(HALO, NX)] = mine[...]

    r_high, r_low = split(rot[...])
    r_both = jnp.concatenate([r_high, r_low], 0)
    for j in range(0, NORB, 2):
        base = (j // 8) * 128
        shape = (128, 256)
        pick = indicator(
            shape, lambda r: r + base, lambda c: (j + (c >> 7)) * NB + (c & (NB - 1))
        )
        both = dot_nn(r_both[:, base : base + 128], jnp.where(pick, 1.0, 0.0).astype(BF))
        both = both[:NB] + both[NB:]
        own = indicator((NB, 256), lambda r: r & 7, lambda c: (c & 127) >> 4)
        both = jnp.where(own, both, 0.0).reshape(2, 8, 256).sum(1)
        packed[j] = both[:, :128]
        packed[j + 1] = both[:, 128:]
    panels[orb] = packed[orb]
    greet(1)
    field = act[pl.ds(HALO, NX)]
    inner = (pot[...] - 1.5 * CENTER) * field
    for k in range(1, 7):
        near = (
            pltpu.roll(field, k, 1) + pltpu.roll(field, NY - k, 1)
            + pltpu.roll(field, k, 2) + pltpu.roll(field, NZ - k, 2)
        )
        inner = inner - (0.5 * SIDES[k - 1]) * near
    greet(2)
    arrive(others)
    for j in range(2):
        def cast(a, carry, j=j):
            high, low = split(x2[j, a])
            xh[j, a] = high
            xl[j, a] = low
            return carry
        lax.fori_loop(0, NB, cast, 0)
    arrive(halo)
    for k in range(1, 7):
        inner = inner - (0.5 * SIDES[k - 1]) * (act[pl.ds(HALO + k, NX)] + act[pl.ds(HALO - k, NX)])
    amat[z] = inner

    cols = 2 * NB * NY

    def shard(k):
        return amat.at[chip(k)]

    def same_y(rows):
        return indicator((rows, cols), lambda r: r & (NY - 1), lambda c: c & (NY - 1))

    def x_pairs():
        for x in range(0, NX, 2):
            yield x, *(
                jnp.concatenate([r[:, :, x].reshape(cols, NZ), r[:, :, x + 1].reshape(cols, NZ)], 1)
                for r in (xh, xl)
            )

    def project(batch, ks):
        rows = len(ks) * NY
        gram = jnp.zeros((rows, cols), F32)
        for x, h_pair, l_pair in x_pairs():
            a_pair = jnp.concatenate([
                jnp.concatenate([shard(k)[x] for k in ks], 0),
                jnp.concatenate([shard(k)[x + 1] for k in ks], 0),
            ], 1)
            a_high, a_low = split(a_pair)
            both = dot_nt(jnp.concatenate([a_high, a_low], 0), h_pair)
            gram = gram + (both[:rows] + both[rows:] + dot_nt(a_high, l_pair))
        summed = jnp.where(same_y(rows), gram, 0.0).reshape(len(ks), NY, cols).sum(1)
        summed = jnp.concatenate([summed, jnp.zeros((4 - len(ks), cols), F32)], 0)
        of_orbital = indicator((cols, 128), lambda r: r >> 4, lambda c: c)
        s_both = jnp.concatenate(split(summed), 0)
        summed = dot_nn(s_both, jnp.where(of_orbital, 1.0, 0.0).astype(BF))
        pbuf[batch, dom] = summed[:4] + summed[4:]
        ref = pbuf.at[batch, dom]
        sums = new(pbuf.at[batch, pl.ds(0, NDOM - 1)])
        sent[6 + batch]["span"] = sums["span"]
        for k in range(1, NDOM):
            remote(ref, ref, side(k), sums, sent[6 + batch])
        return sums

    def remove(batch, ks, copies, halves):
        rows = len(ks) * NY
        arrive(copies)
        proj = pbuf[batch].sum(0) * (1.0 / (NX * NDOM * NY * NZ))
        to_rows = indicator((128, cols), lambda r: r, lambda c: c >> 4)
        spread = dot_nn(
            jnp.concatenate(split(proj), 0), jnp.where(to_rows, 1.0, 0.0).astype(BF)
        )
        keep = same_y(rows)
        weights = []
        for first in (0, 4):
            one = spread[first : first + len(ks)]
            one = jnp.broadcast_to(one[:, None, :], (len(ks), NY, cols)).reshape(rows, cols)
            weights.append(jnp.where(keep, one, 0.0).astype(BF))
        k_both = jnp.concatenate(weights, 0)
        for x, h_pair, l_pair in x_pairs():
            both = dot_nn(k_both, h_pair)
            part = both[:rows] + both[rows:] + dot_nn(weights[0], l_pair)
            for i, k in enumerate(ks):
                remo[chip(k), x] = part[i * NY : (i + 1) * NY, :NZ]
                remo[chip(k), x + 1] = part[i * NY : (i + 1) * NY, NZ:]
            if x == 2 or x == 6:
                halves(x // 4)

    phase[0] = 2
    one, on = new(), new()
    gather_one(shard, 0, one)
    gather_one(shard, 1, one)
    two = [gather_two(shard, 0), gather_two(shard, 1)]
    greet(3)
    arrive(one)
    batches = ((0, 1, -1), (2, -2), (3, -3, 4))
    sums = [project(0, batches[0])]
    gather_on(shard, 0, two[0], on, on)
    gather_on(shard, 1, two[1], on, on)
    sums.append(project(1, batches[1]))

    def removed(k):
        return remo.at[chip(k + 4)]

    def owned(k):
        return grad.at[2 * chip(k + 4) + q]

    phase[0] = 3
    far, last, twins = [], [new(), new()], [new(), new()]
    remove(0, batches[0], sums[0], lambda h: far.append(scatter_far(removed, 1, h)))
    arrive(on)
    sums.append(project(2, batches[2]))
    panel_copies = new(panels.at[pl.ds(0, NORB - 1)])
    sent[5]["span"] = panel_copies["span"]
    for k in range(1, NORB):
        to = lax.rem(orb + k, NORB)
        remote(packed.at[to], panels.at[orb], (dom, to), panel_copies, sent[5])
    remove(1, batches[1], sums[1], lambda h: None)
    for h in range(2):
        scatter_mid(removed, 1, h, far[h], last[h])
    remove(2, batches[2], sums[2], lambda h: scatter_near(removed, 1, h, last[h]))

    phase[0] = 4

    def to_sibling(k, h):
        ref = owned(k).at[pl.ds(4 * h, 4)]
        remote(ref, ref, sibling, twins[h])

    two, one, three, four = [], [new(), new()], [new(), new()], [new(), new()]
    for h in range(2):
        half = pl.ds(4 * h, 4)
        owned(0)[half] = amat[chip(4), half] - scatter_sum(removed, 1, h, last[h])
        two.append(gather_two(owned, h))
        gather_one(owned, h, one[h])
        to_sibling(0, h)

    arrive(panel_copies)
    rows = NB * NY
    panel = panels[owner_ref[0]]
    panel = jnp.broadcast_to(panel[:, None, :], (2, 8, 128)).reshape(NB, 128)
    own = indicator((NB, 128), lambda r: r & 7, lambda c: c >> 4)
    p_both = jnp.concatenate(split(jnp.where(own, panel, 0.0)), 0)
    of_column = indicator((rows, 128), lambda r: r >> 4, lambda c: c & (NB - 1))
    by_row = dot_nt(jnp.where(of_column, 1.0, 0.0).astype(BF), p_both).astype(BF)
    to_rows = indicator((NB, rows), lambda r: r, lambda c: c >> 4)
    to_rows = jnp.where(to_rows, 1.0, 0.0).astype(BF)
    keep = indicator((rows, rows), lambda r: r & (NY - 1), lambda c: c & (NY - 1))
    w_high, w_low = (
        jnp.where(keep, dot_nn(one_of, to_rows), 0.0).astype(BF)
        for one_of in (by_row[:, :NB], by_row[:, NB:])
    )
    w_both = jnp.concatenate([w_high, w_low], 0)

    w_ref[...] = w_both
    upd[:, 4:] = x2[q, :, 4:]

    for h in range(2):
        gather_on(owned, h, two[h], three[h], four[h], to_sibling)
    for h in range(2):
        arrive(one[h])
        to_sibling(-1, h)
        to_sibling(1, h)
    for h in range(2):
        arrive(three[h])
        to_sibling(-3, h)
        to_sibling(3, h)
        arrive(four[h])
        to_sibling(4, h)

    arrive(twins[0])
    for x in range(0, 4, 2):
        update(grad, w_both, x2.at[q], upd, x, x)
    arrive(twins[1])
    for group in sent:
        span(group).wait_send()
    assert next(groups) == recv.shape[0]


def update(grad, w_both, old, new, x, at):
    rows = NB * NY
    g_pair = jnp.concatenate([grad[:, x].reshape(rows, NZ), grad[:, x + 1].reshape(rows, NZ)], 1)
    g_high, g_low = split(g_pair)
    both = dot_nn(w_both, g_high)
    part = both[:rows] + both[rows:] + dot_nn(w_both[:rows], g_low)
    new[:, at] = old[:, x] + part[:, :NZ].reshape(NB, NY, NZ)
    new[:, at + 1] = old[:, x + 1] + part[:, NZ:].reshape(NB, NY, NZ)


def update_kernel(grad, w_ref, upd, grad_hbm, upd_hbm, done, sem):
    outs = []

    def out(src, dst):
        outs.append(pltpu.make_async_copy(src, dst, sem.at[len(outs)]))
        outs[-1].start()

    out(upd.at[:, pl.ds(0, 4)], upd_hbm.at[:, pl.ds(0, 4)])
    out(grad, grad_hbm)
    w_both = w_ref[...]
    for x in range(4, NX, 2):
        pair = pl.ds(x, 2)
        update(grad, w_both, upd, done, x, x - 4)
        out(done.at[:, pl.ds(x - 4, 2)], upd_hbm.at[:, pair])
    for copy in outs:
        copy.wait()


def per_device(orbitals, potential, rotation, block, owner):
    shard = (NX, NY, NZ)
    scratch = [
        pltpu.VMEM((2, NB, *shard), F32),
        pltpu.VMEM((2, NB, *shard), BF),
        pltpu.VMEM((2, NB, *shard), BF),
        pltpu.VMEM(shard, F32),
        pltpu.VMEM((NB, NB * NORB), F32),
        pltpu.VMEM((NCHIP, *shard), F32),
        pltpu.VMEM((NX + 2 * HALO, NY, NZ), F32),
        pltpu.VMEM((NCHIP, *shard), F32),
        pltpu.VMEM((3, NDOM, 4, 128), F32),
        pltpu.VMEM((NORB, 2, 128), F32),
        pltpu.VMEM((NORB, 2, 128), F32),
        pltpu.VMEM((2, 2, *shard), F32),
        pltpu.VMEM((2, 2, *shard), F32),
        pltpu.VMEM((2, 2, *shard), F32),
        pltpu.VMEM((2, 2, *shard), F32),
        pltpu.VMEM((2, 2, *shard), F32),
        pltpu.SemaphoreType.DMA((9,)),
        pltpu.SemaphoreType.DMA((30,)),
        pltpu.SemaphoreType.DMA((3,)),
        pltpu.SemaphoreType.REGULAR((3,)),
    ]
    hbm = pl.BlockSpec(memory_space=pl.ANY)
    smem = pl.BlockSpec(memory_space=pltpu.SMEM)
    vmem = pl.BlockSpec(memory_space=pltpu.VMEM)
    whole = jax.ShapeDtypeStruct((NB, *shard), F32)
    x_hbm = pltpu.with_memory_space_constraint(orbitals, pltpu.HBM)
    arrays = (pltpu.with_memory_space_constraint(v, pltpu.HBM) for v in (potential, rotation))
    mine = lax.switch(block[0], [functools.partial(scattered, r) for r in range(NORB)], x_hbm)
    gradient, weights, updated = pl.pallas_call(
        kernel,
        out_shape=(whole, jax.ShapeDtypeStruct((2 * NB * NY, NB * NY), BF), whole),
        in_specs=[smem, vmem, hbm, hbm, hbm],
        out_specs=(vmem, vmem, vmem),
        scratch_shapes=scratch,
        compiler_params=pltpu.CompilerParams(
            collective_id=NORB, has_side_effects=True, vmem_limit_bytes=40 << 20
        ),
        cost_estimate=pl.CostEstimate(flops=1 << 28, bytes_accessed=3 << 20, transcendentals=0),
        name="gradient",
    )(owner, mine, x_hbm, *arrays)
    return pl.pallas_call(
        update_kernel,
        out_shape=(whole, whole),
        in_specs=[vmem, vmem, vmem],
        out_specs=(hbm, hbm),
        scratch_shapes=[
            pltpu.VMEM((NB, NX // 2, NY, NZ), F32),
            pltpu.SemaphoreType.DMA((4,)),
        ],
        compiler_params=pltpu.CompilerParams(vmem_limit_bytes=16 << 20),
        cost_estimate=pl.CostEstimate(flops=1 << 28, bytes_accessed=4 << 20, transcendentals=0),
        name="update",
    )(gradient, weights, updated)


def solution(mesh):
    in_specs = (P("orb", "dom", None, None), P("dom", None, None), P("orb", None), P(), P())
    out_specs = (P(None, "dom", None, None), P("orb", "dom", None, None))
    return jax.shard_map(
        per_device, mesh=mesh, in_specs=in_specs, out_specs=out_specs, check_vma=False
    )
```

```python
import itertools
import math

import jax
import jax.numpy as jnp
from jax import lax
from jax.experimental import pallas as pl
from jax.experimental.pallas import tpu as pltpu
from jax.sharding import PartitionSpec as P

CENTER = -5369.0 / 1800.0
SIDES = (12.0 / 7.0, -15.0 / 56.0, 10.0 / 189.0, -1.0 / 112.0, 2.0 / 1925.0, -1.0 / 16632.0)

MESH = pl.DeviceIdType.MESH
NB = 16
NX, NY, NZ = 8, 16, 128
NDOM, NORB, NCHIP = 16, 16, 8
HALO = 6
BF = jnp.bfloat16
F32 = jnp.float32


def split(value):
    high = value.astype(BF)
    return high, (value - high.astype(F32)).astype(BF)


def dot_nt(a, b):
    return lax.dot_general(a, b, (((1,), (1,)), ((), ())), preferred_element_type=F32)


def dot_nn(a, b):
    return lax.dot_general(a, b, (((1,), (0,)), ((), ())), preferred_element_type=F32)


def indicator(shape, row_of, col_of):
    rows = lax.broadcasted_iota(jnp.int32, shape, 0)
    cols = lax.broadcasted_iota(jnp.int32, shape, 1)
    return row_of(rows) == col_of(cols)


def kernel(
    block_ref, owner_ref, x_hbm, pot_hbm, rot_hbm, grad, w_ref, upd,
    x2, xh, xl, pot, rot, mask, remo, act, ham, amat, pout, pbuf, packed, panels,
    a1, a2, d1, b2, sb, send, recv, loc,
):
    dom = lax.axis_index("dom")
    orb = lax.axis_index("orb")
    z = lax.div(orb, 2)
    q = lax.rem(orb, 2)

    def chip(k):
        return lax.rem(z + (k + 2 * NCHIP), NCHIP)

    def peer(k):
        return (dom, 2 * chip(k) + q)

    def side(k):
        return (lax.rem(dom + (k + NDOM), NDOM), orb)

    twin = orb + 1 - 2 * q
    sibling = (dom, twin)

    def across(k):
        return (lax.rem(dom + k, NDOM), twin)
    groups = itertools.count()
    sent = [dict(sem=i, rows=0) for i in range(send.shape[0])]
    phase = [0]

    def new(span=None):
        return dict(sem=next(groups), rows=0, span=span)

    def remote(src, dst, device, group, sends=None):
        sends = sent[phase[0]] if sends is None else sends
        pltpu.make_async_remote_copy(
            src_ref=src, dst_ref=dst, send_sem=send.at[sends["sem"]], recv_sem=recv.at[group["sem"]],
            device_id=device, device_id_type=MESH,
        ).start()
        for one in (group, sends):
            one["rows"] += math.prod(src.shape[:-1])

    def span(group):
        planes = group["rows"] // NY
        if group.get("span") is not None:
            ref = group["span"]
        elif planes <= act.shape[0]:
            ref = act.at[pl.ds(0, planes)]
        else:
            ref = x2.at[0, pl.ds(0, planes // NX)]
        assert math.prod(ref.shape[:-1]) == group["rows"]
        return pltpu.make_async_remote_copy(
            src_ref=ref, dst_ref=ref, send_sem=send.at[group["sem"] % len(sent)],
            recv_sem=recv.at[group["sem"]], device_id=sibling, device_id_type=MESH,
        )

    def arrive(*waited):
        for group in waited:
            span(group).wait_recv()

    loads = [
        pltpu.make_async_copy(src, dst, loc.at[i])
        for i, (src, dst) in enumerate(((x_hbm, x2.at[q]), (pot_hbm, pot), (rot_hbm, rot)))
    ]
    loads[0].start()
    barrier = pltpu.get_barrier_semaphore()
    for k in (8, 9, 7, 10, 6, 11, 5, 12, 4, 13, 3, 14, 2, 15, 1):
        pl.semaphore_signal(
            barrier, inc=1, device_id=(dom, lax.rem(orb + k, NORB)), device_id_type=MESH
        )
    for k in range(1, NDOM):
        pl.semaphore_signal(barrier, inc=1, device_id=across(k), device_id_type=MESH)
    for k in (1, -1):
        pl.semaphore_signal(barrier, inc=1, device_id=side(k), device_id_type=MESH)
    for copy in loads[1:]:
        copy.start()
    for copy in loads:
        copy.wait()
    pl.semaphore_wait(barrier, NDOM + NORB)

    def scatter_far(part, slot, h):
        whole, front, back = pl.ds(4 * h, 4), pl.ds(4 * h, 2), pl.ds(4 * h + 2, 2)
        up, down = new(), new()
        remote(part(4).at[front], a2.at[slot, 0, front], peer(2), up)
        remote(part(4).at[back], a2.at[slot, 1, back], peer(-2), down)
        remote(part(3).at[whole], a1.at[slot, 0, whole], peer(1), up)
        remote(part(-3).at[whole], a1.at[slot, 1, whole], peer(-1), down)
        return up, down

    def scatter_mid(part, slot, h, far, last):
        whole, front, back = pl.ds(4 * h, 4), pl.ds(4 * h, 2), pl.ds(4 * h + 2, 2)
        for i, sign, quarter in ((0, 1, front), (1, -1, back)):
            arrive(far[i])
            sb[slot, i, whole] = part(2 * sign)[whole] + a1[slot, i, whole]
            sb[slot, i, quarter] = sb[slot, i, quarter] + a2[slot, i, quarter]
            remote(sb.at[slot, i, whole], b2.at[slot, i, whole], peer(2 * sign), last)

    def scatter_near(part, slot, h, last):
        whole = pl.ds(4 * h, 4)
        remote(part(1).at[whole], d1.at[slot, 0, whole], peer(1), last)
        remote(part(-1).at[whole], d1.at[slot, 1, whole], peer(-1), last)

    def scatter_sum(part, slot, h, last):
        whole = pl.ds(4 * h, 4)
        arrive(last)
        return (
            part(0)[whole]
            + (d1[slot, 0, whole] + d1[slot, 1, whole])
            + (b2[slot, 0, whole] + b2[slot, 1, whole])
        )

    def give(shard, k, to, planes, group):
        ref = shard(k).at[planes]
        remote(ref, ref, peer(to), group)

    def gather_two(shard, h):
        whole = pl.ds(4 * h, 4)
        two = new(), new()
        give(shard, 0, 2, whole, two[0])
        give(shard, 0, -2, whole, two[1])
        return two

    def gather_one(shard, h, group):
        whole = pl.ds(4 * h, 4)
        give(shard, 0, 1, whole, group)
        give(shard, 0, -1, whole, group)

    def gather_on(shard, h, two, three, four, arrived=lambda k, h: None):
        whole, front, back = pl.ds(4 * h, 4), pl.ds(4 * h, 2), pl.ds(4 * h + 2, 2)
        arrive(two[0])
        give(shard, -2, 2, front, four)
        give(shard, -2, 1, whole, three)
        arrived(-2, h)
        arrive(two[1])
        give(shard, 2, -2, back, four)
        give(shard, 2, -1, whole, three)
        arrived(2, h)

    order = (4, 3, -3, 2, -2, 1, -1, 0)

    def to_twin(ks, parity):
        group = new()
        for k in ks:
            ref = x2.at[q, 2 * chip(k) + parity]
            remote(ref, ref, sibling, group)
        return group

    wanted = to_twin(order[:3], 1 - q), to_twin(order[3:], 1 - q)

    block = block_ref[0]
    root_core = lax.rem(block, 2)
    is_root = lax.div(block, 2) == z

    def masked(k):
        return mask.at[chip(k)]

    def fill(ks, copies):
        arrive(copies)
        for k in ks:
            i = 2 * chip(k) + q
            mine = jnp.where(root_core == 0, x2[0, i], x2[1, i])
            mask[chip(k)] = jnp.where(is_root, mine, 0.0)

    fill(order[:3], wanted[0])
    phase[0] = 1
    far = [scatter_far(masked, 0, h) for h in range(2)]
    fill(order[3:], wanted[1])
    last = [new(), new()]
    for h in range(2):
        scatter_near(masked, 0, h, last[h])
    others = to_twin(order, q)
    for h in range(2):
        scatter_mid(masked, 0, h, far[h], last[h])

    phase[0] = 2
    halo = new()

    def lend(first, planes, to, shift):
        src, dst = act.at[pl.ds(first, planes)], act.at[pl.ds(first + shift, planes)]
        remote(src, dst, side(to), halo)

    act[pl.ds(HALO, 4)] = scatter_sum(masked, 0, 0, last[0])
    lend(HALO, 4, -1, NX)
    lend(HALO + 2, 2, 1, -NX)
    act[pl.ds(HALO + 4, 4)] = scatter_sum(masked, 0, 1, last[1])
    lend(HALO + 4, 2, -1, NX)
    lend(HALO + 4, 4, 1, -NX)

    r_high, r_low = split(rot[...])
    r_both = jnp.concatenate([r_high, r_low], 0)
    for j in range(0, NORB, 2):
        base = (j // 8) * 128
        shape = (128, 256)
        pick = indicator(
            shape, lambda r: r + base, lambda c: (j + (c >> 7)) * NB + (c & (NB - 1))
        )
        both = dot_nn(r_both[:, base : base + 128], jnp.where(pick, 1.0, 0.0).astype(BF))
        both = both[:NB] + both[NB:]
        own = indicator((NB, 256), lambda r: r & 7, lambda c: (c & 127) >> 4)
        both = jnp.where(own, both, 0.0).reshape(2, 8, 256).sum(1)
        packed[j] = both[:, :128]
        packed[j + 1] = both[:, 128:]
    panels[orb] = packed[orb]
    panel_copies = new(panels.at[pl.ds(0, NORB - 1)])
    sent[6]["span"] = panel_copies["span"]
    for k in range(1, NORB):
        to = lax.rem(orb + k, NORB)
        remote(packed.at[to], panels.at[orb], (dom, to), panel_copies, sent[6])

    field = act[pl.ds(HALO, NX)]
    inner = (pot[...] - 1.5 * CENTER) * field
    for k in range(1, 7):
        near = (
            pltpu.roll(field, k, 1) + pltpu.roll(field, NY - k, 1)
            + pltpu.roll(field, k, 2) + pltpu.roll(field, NZ - k, 2)
        )
        inner = inner - (0.5 * SIDES[k - 1]) * near
    arrive(others)
    for j in range(2):
        def cast(a, carry, j=j):
            high, low = split(x2[j, a])
            xh[j, a] = high
            xl[j, a] = low
            return carry
        lax.fori_loop(0, NB, cast, 0)
    arrive(halo)
    for k in range(1, 7):
        inner = inner - (0.5 * SIDES[k - 1]) * (act[pl.ds(HALO + k, NX)] + act[pl.ds(HALO - k, NX)])
    amat[z] = inner

    cols = 2 * NB * NY

    def shard(k):
        return amat.at[chip(k)]

    def same_y(rows):
        return indicator((rows, cols), lambda r: r & (NY - 1), lambda c: c & (NY - 1))

    def x_pairs():
        for x in range(0, NX, 2):
            yield x, *(
                jnp.concatenate([r[:, :, x].reshape(cols, NZ), r[:, :, x + 1].reshape(cols, NZ)], 1)
                for r in (xh, xl)
            )

    def project(batch, ks):
        rows = len(ks) * NY
        gram = jnp.zeros((rows, cols), F32)
        for x, h_pair, l_pair in x_pairs():
            a_pair = jnp.concatenate([
                jnp.concatenate([shard(k)[x] for k in ks], 0),
                jnp.concatenate([shard(k)[x + 1] for k in ks], 0),
            ], 1)
            a_high, a_low = split(a_pair)
            both = dot_nt(jnp.concatenate([a_high, a_low], 0), h_pair)
            gram = gram + (both[:rows] + both[rows:] + dot_nt(a_high, l_pair))
        summed = jnp.where(same_y(rows), gram, 0.0).reshape(len(ks), NY, cols).sum(1)
        summed = jnp.concatenate([summed, jnp.zeros((4 - len(ks), cols), F32)], 0)
        of_orbital = indicator((cols, 128), lambda r: r >> 4, lambda c: c)
        s_both = jnp.concatenate(split(summed), 0)
        summed = dot_nn(s_both, jnp.where(of_orbital, 1.0, 0.0).astype(BF))
        pout[batch] = summed[:4] + summed[4:]
        sums = new(pbuf.at[batch])
        sent[7 + batch]["span"] = sums["span"]
        for k in range(NDOM):
            remote(pout.at[batch], pbuf.at[batch, dom], across(k), sums, sent[7 + batch])
        return sums

    def remove(batch, ks, copies, halves):
        rows = len(ks) * NY
        arrive(copies)
        proj = pbuf[batch].sum(0) * (1.0 / (NX * NDOM * NY * NZ))
        to_rows = indicator((128, cols), lambda r: r, lambda c: c >> 4)
        spread = dot_nn(
            jnp.concatenate(split(proj), 0), jnp.where(to_rows, 1.0, 0.0).astype(BF)
        )
        keep = same_y(rows)
        weights = []
        for first in (0, 4):
            one = spread[first : first + len(ks)]
            one = jnp.broadcast_to(one[:, None, :], (len(ks), NY, cols)).reshape(rows, cols)
            weights.append(jnp.where(keep, one, 0.0).astype(BF))
        k_both = jnp.concatenate(weights, 0)
        for x, h_pair, l_pair in x_pairs():
            both = dot_nn(k_both, h_pair)
            part = both[:rows] + both[rows:] + dot_nn(weights[0], l_pair)
            for i, k in enumerate(ks):
                remo[chip(k), x] = part[i * NY : (i + 1) * NY, :NZ]
                remo[chip(k), x + 1] = part[i * NY : (i + 1) * NY, NZ:]
            if x == 2 or x == 6:
                halves(x // 4)

    phase[0] = 3
    one, on = new(), new()
    gather_one(shard, 0, one)
    gather_one(shard, 1, one)
    two = [gather_two(shard, 0), gather_two(shard, 1)]
    arrive(one)
    batches = ((0, 1, -1), (2, -2), (3, -3, 4))
    sums = [project(0, batches[0])]
    gather_on(shard, 0, two[0], on, on)
    gather_on(shard, 1, two[1], on, on)
    sums.append(project(1, batches[1]))

    def removed(k):
        return remo.at[chip(k + 4)]

    def owned(k):
        return grad.at[2 * chip(k + 4) + 1 - q]

    phase[0] = 4
    far, last, twins = [], [new(), new()], [new(), new()]
    remove(0, batches[0], sums[0], lambda h: far.append(scatter_far(removed, 1, h)))
    arrive(on)
    base = new()
    remote(shard(4), ham, sibling, base)
    sums.append(project(2, batches[2]))
    remove(1, batches[1], sums[1], lambda h: None)
    for h in range(2):
        scatter_mid(removed, 1, h, far[h], last[h])
    remove(2, batches[2], sums[2], lambda h: scatter_near(removed, 1, h, last[h]))

    phase[0] = 5

    def to_sibling(k, h):
        ref = owned(k).at[pl.ds(4 * h, 4)]
        remote(ref, ref, sibling, twins[h])

    arrive(base)
    two, one, three, four = [], [new(), new()], [new(), new()], [new(), new()]
    for h in range(2):
        half = pl.ds(4 * h, 4)
        owned(0)[half] = ham[half] - scatter_sum(removed, 1, h, last[h])
        two.append(gather_two(owned, h))
        gather_one(owned, h, one[h])
        to_sibling(0, h)

    arrive(panel_copies)
    rows = NB * NY
    panel = panels[owner_ref[0]]
    panel = jnp.broadcast_to(panel[:, None, :], (2, 8, 128)).reshape(NB, 128)
    own = indicator((NB, 128), lambda r: r & 7, lambda c: c >> 4)
    p_both = jnp.concatenate(split(jnp.where(own, panel, 0.0)), 0)
    of_column = indicator((rows, 128), lambda r: r >> 4, lambda c: c & (NB - 1))
    by_row = dot_nt(jnp.where(of_column, 1.0, 0.0).astype(BF), p_both).astype(BF)
    to_rows = indicator((NB, rows), lambda r: r, lambda c: c >> 4)
    to_rows = jnp.where(to_rows, 1.0, 0.0).astype(BF)
    keep = indicator((rows, rows), lambda r: r & (NY - 1), lambda c: c & (NY - 1))
    w_high, w_low = (
        jnp.where(keep, dot_nn(one_of, to_rows), 0.0).astype(BF)
        for one_of in (by_row[:, :NB], by_row[:, NB:])
    )
    w_both = jnp.concatenate([w_high, w_low], 0)

    w_ref[...] = w_both
    upd[:, 4:] = x2[q, :, 4:]

    for h in range(2):
        gather_on(owned, h, two[h], three[h], four[h], to_sibling)
    for h in range(2):
        arrive(one[h])
        to_sibling(-1, h)
        to_sibling(1, h)
    for h in range(2):
        arrive(three[h])
        to_sibling(-3, h)
        to_sibling(3, h)
        arrive(four[h])
        to_sibling(4, h)

    arrive(twins[0])
    for x in range(0, 4, 2):
        update(grad, w_both, x2.at[q], upd, x, x)
    arrive(twins[1])
    for group in sent:
        span(group).wait_send()
    assert next(groups) == recv.shape[0]


def update(grad, w_both, old, new, x, at):
    rows = NB * NY
    g_pair = jnp.concatenate([grad[:, x].reshape(rows, NZ), grad[:, x + 1].reshape(rows, NZ)], 1)
    g_high, g_low = split(g_pair)
    both = dot_nn(w_both, g_high)
    part = both[:rows] + both[rows:] + dot_nn(w_both[:rows], g_low)
    new[:, at] = old[:, x] + part[:, :NZ].reshape(NB, NY, NZ)
    new[:, at + 1] = old[:, x + 1] + part[:, NZ:].reshape(NB, NY, NZ)


def update_kernel(grad, w_ref, upd, grad_hbm, upd_hbm, done, sem):
    outs = []

    def out(src, dst):
        outs.append(pltpu.make_async_copy(src, dst, sem.at[len(outs)]))
        outs[-1].start()

    out(upd.at[:, pl.ds(0, 4)], upd_hbm.at[:, pl.ds(0, 4)])
    out(grad, grad_hbm)
    w_both = w_ref[...]
    for x in range(4, NX, 2):
        pair = pl.ds(x, 2)
        update(grad, w_both, upd, done, x, x - 4)
        out(done.at[:, pl.ds(x - 4, 2)], upd_hbm.at[:, pair])
    for copy in outs:
        copy.wait()


def per_device(orbitals, potential, rotation, block, owner):
    shard = (NX, NY, NZ)
    scratch = [
        pltpu.VMEM((2, NB, *shard), F32),
        pltpu.VMEM((2, NB, *shard), BF),
        pltpu.VMEM((2, NB, *shard), BF),
        pltpu.VMEM(shard, F32),
        pltpu.VMEM((NB, NB * NORB), F32),
        pltpu.VMEM((NCHIP, *shard), F32),
        pltpu.VMEM((NCHIP, *shard), F32),
        pltpu.VMEM((NX + 2 * HALO, NY, NZ), F32),
        pltpu.VMEM(shard, F32),
        pltpu.VMEM((NCHIP, *shard), F32),
        pltpu.VMEM((3, 4, 128), F32),
        pltpu.VMEM((3, NDOM, 4, 128), F32),
        pltpu.VMEM((NORB, 2, 128), F32),
        pltpu.VMEM((NORB, 2, 128), F32),
        pltpu.VMEM((2, 2, *shard), F32),
        pltpu.VMEM((2, 2, *shard), F32),
        pltpu.VMEM((2, 2, *shard), F32),
        pltpu.VMEM((2, 2, *shard), F32),
        pltpu.VMEM((2, 2, *shard), F32),
        pltpu.SemaphoreType.DMA((10,)),
        pltpu.SemaphoreType.DMA((39,)),
        pltpu.SemaphoreType.DMA((3,)),
    ]
    hbm = pl.BlockSpec(memory_space=pl.ANY)
    smem = pl.BlockSpec(memory_space=pltpu.SMEM)
    vmem = pl.BlockSpec(memory_space=pltpu.VMEM)
    whole = jax.ShapeDtypeStruct((NB, *shard), F32)
    arrays = (pltpu.with_memory_space_constraint(v, pltpu.HBM) for v in (orbitals, potential, rotation))
    gradient, weights, updated = pl.pallas_call(
        kernel,
        out_shape=(whole, jax.ShapeDtypeStruct((2 * NB * NY, NB * NY), BF), whole),
        in_specs=[smem, smem, hbm, hbm, hbm],
        out_specs=(vmem, vmem, vmem),
        scratch_shapes=scratch,
        compiler_params=pltpu.CompilerParams(
            collective_id=0, has_side_effects=True, vmem_limit_bytes=40 << 20
        ),
        cost_estimate=pl.CostEstimate(flops=1 << 28, bytes_accessed=3 << 20, transcendentals=0),
        name="gradient",
    )(block, owner, *arrays)
    return pl.pallas_call(
        update_kernel,
        out_shape=(whole, whole),
        in_specs=[vmem, vmem, vmem],
        out_specs=(hbm, hbm),
        scratch_shapes=[
            pltpu.VMEM((NB, NX // 2, NY, NZ), F32),
            pltpu.SemaphoreType.DMA((4,)),
        ],
        compiler_params=pltpu.CompilerParams(vmem_limit_bytes=16 << 20),
        cost_estimate=pl.CostEstimate(flops=1 << 28, bytes_accessed=4 << 20, transcendentals=0),
        name="update",
    )(gradient, weights, updated)


def solution(mesh):
    in_specs = (P("orb", "dom", None, None), P("dom", None, None), P("orb", None), P(), P())
    out_specs = (P(None, "dom", None, None), P("orb", "dom", None, None))
    return jax.shard_map(
        per_device, mesh=mesh, in_specs=in_specs, out_specs=out_specs, check_vma=False
    )
```

```python
import itertools
import math

import jax
import jax.numpy as jnp
from jax import lax
from jax.experimental import pallas as pl
from jax.experimental.pallas import tpu as pltpu
from jax.sharding import PartitionSpec as P

CENTER = -5369.0 / 1800.0
SIDES = (12.0 / 7.0, -15.0 / 56.0, 10.0 / 189.0, -1.0 / 112.0, 2.0 / 1925.0, -1.0 / 16632.0)

MESH = pl.DeviceIdType.MESH
NB = 16
NX, NY, NZ = 8, 16, 128
NDOM, NORB, NCHIP = 16, 16, 8
HALO = 6
BF = jnp.bfloat16
F32 = jnp.float32


def split(value):
    high = value.astype(BF)
    return high, (value - high.astype(F32)).astype(BF)


def dot_nt(a, b):
    return lax.dot_general(a, b, (((1,), (1,)), ((), ())), preferred_element_type=F32)


def dot_nn(a, b):
    return lax.dot_general(a, b, (((1,), (0,)), ((), ())), preferred_element_type=F32)


def indicator(shape, row_of, col_of):
    rows = lax.broadcasted_iota(jnp.int32, shape, 0)
    cols = lax.broadcasted_iota(jnp.int32, shape, 1)
    return row_of(rows) == col_of(cols)


def kernel(
    block_ref, owner_ref, x_hbm, pot_hbm, rot_hbm, grad, w_ref, upd,
    x2, xh, xl, pot, rot, mask, remo, act, ham, amat, pout, pbuf, packed, panels,
    a1, a2, d1, b2, sb, send, recv, loc, greetings,
):
    dom = lax.axis_index("dom")
    orb = lax.axis_index("orb")
    z = lax.div(orb, 2)
    q = lax.rem(orb, 2)

    def chip(k):
        return lax.rem(z + (k + 2 * NCHIP), NCHIP)

    def peer(k):
        return (dom, 2 * chip(k) + q)

    def side(k):
        return (lax.rem(dom + (k + NDOM), NDOM), orb)

    twin = orb + 1 - 2 * q
    sibling = (dom, twin)

    def across(k):
        return (lax.rem(dom + k, NDOM), twin)
    groups = itertools.count()
    sent = [dict(sem=i, rows=0) for i in range(send.shape[0])]
    phase = [0]

    def new(span=None):
        return dict(sem=next(groups), rows=0, span=span)

    def remote(src, dst, device, group, sends=None):
        sends = sent[phase[0]] if sends is None else sends
        pltpu.make_async_remote_copy(
            src_ref=src, dst_ref=dst, send_sem=send.at[sends["sem"]], recv_sem=recv.at[group["sem"]],
            device_id=device, device_id_type=MESH,
        ).start()
        for one in (group, sends):
            one["rows"] += math.prod(src.shape[:-1])

    def span(group):
        planes = group["rows"] // NY
        if group.get("span") is not None:
            ref = group["span"]
        elif planes <= act.shape[0]:
            ref = act.at[pl.ds(0, planes)]
        else:
            ref = x2.at[0, pl.ds(0, planes // NX)]
        assert math.prod(ref.shape[:-1]) == group["rows"]
        return pltpu.make_async_remote_copy(
            src_ref=ref, dst_ref=ref, send_sem=send.at[group["sem"] % len(sent)],
            recv_sem=recv.at[group["sem"]], device_id=sibling, device_id_type=MESH,
        )

    def arrive(*waited):
        for group in waited:
            span(group).wait_recv()

    loads = [
        pltpu.make_async_copy(src, dst, loc.at[i])
        for i, (src, dst) in enumerate(((x_hbm, x2.at[q]), (pot_hbm, pot), (rot_hbm, rot)))
    ]
    loads[0].start()
    row, col = lax.div(dom, 4), lax.rem(dom, 4)
    around = [
        (4 * lax.rem(row + i, 4) + lax.rem(col + j, 4), orb) for i, j in ((0, 1), (0, 3), (1, 0), (3, 0))
    ]
    near = [peer(2), peer(-2), peer(1), peer(-1), sibling, side(1), side(-1), *around]
    barrier = pltpu.get_barrier_semaphore()
    for device in near:
        pl.semaphore_signal(barrier, inc=1, device_id=device, device_id_type=MESH)
    for copy in loads[1:]:
        copy.start()
    pl.semaphore_wait(barrier, len(near))

    def greet(i):
        if i > 0:
            pl.semaphore_wait(greetings.at[i - 1], len(around))
        if i < 3:
            for device in around:
                pl.semaphore_signal(greetings.at[i], inc=1, device_id=device, device_id_type=MESH)

    def scatter_far(part, slot, h):
        whole, front, back = pl.ds(4 * h, 4), pl.ds(4 * h, 2), pl.ds(4 * h + 2, 2)
        up, down = new(), new()
        remote(part(4).at[front], a2.at[slot, 0, front], peer(2), up)
        remote(part(4).at[back], a2.at[slot, 1, back], peer(-2), down)
        remote(part(3).at[whole], a1.at[slot, 0, whole], peer(1), up)
        remote(part(-3).at[whole], a1.at[slot, 1, whole], peer(-1), down)
        return up, down

    def scatter_mid(part, slot, h, far, last):
        whole, front, back = pl.ds(4 * h, 4), pl.ds(4 * h, 2), pl.ds(4 * h + 2, 2)
        for i, sign, quarter in ((0, 1, front), (1, -1, back)):
            arrive(far[i])
            sb[slot, i, whole] = part(2 * sign)[whole] + a1[slot, i, whole]
            sb[slot, i, quarter] = sb[slot, i, quarter] + a2[slot, i, quarter]
            remote(sb.at[slot, i, whole], b2.at[slot, i, whole], peer(2 * sign), last)

    def scatter_near(part, slot, h, last):
        whole = pl.ds(4 * h, 4)
        remote(part(1).at[whole], d1.at[slot, 0, whole], peer(1), last)
        remote(part(-1).at[whole], d1.at[slot, 1, whole], peer(-1), last)

    def scatter_sum(part, slot, h, last):
        whole = pl.ds(4 * h, 4)
        arrive(last)
        return (
            part(0)[whole]
            + (d1[slot, 0, whole] + d1[slot, 1, whole])
            + (b2[slot, 0, whole] + b2[slot, 1, whole])
        )

    def give(shard, k, to, planes, group):
        ref = shard(k).at[planes]
        remote(ref, ref, peer(to), group)

    def gather_two(shard, h):
        whole = pl.ds(4 * h, 4)
        two = new(), new()
        give(shard, 0, 2, whole, two[0])
        give(shard, 0, -2, whole, two[1])
        return two

    def gather_one(shard, h, group):
        whole = pl.ds(4 * h, 4)
        give(shard, 0, 1, whole, group)
        give(shard, 0, -1, whole, group)

    def gather_on(shard, h, two, three, four, arrived=lambda k, h: None):
        whole, front, back = pl.ds(4 * h, 4), pl.ds(4 * h, 2), pl.ds(4 * h + 2, 2)
        arrive(two[0])
        give(shard, -2, 2, front, four)
        give(shard, -2, 1, whole, three)
        arrived(-2, h)
        arrive(two[1])
        give(shard, 2, -2, back, four)
        give(shard, 2, -1, whole, three)
        arrived(2, h)

    order = (4, 3, -3, 2, -2, 1, -1, 0)

    def to_twin(ks, parity):
        group = new()
        for k in ks:
            i = 2 * chip(k) + parity
            remote(x_hbm.at[i], x2.at[q, i], sibling, group)
        return group

    wanted = to_twin(order[:3], 1 - q), to_twin(order[3:], 1 - q)

    for copy in loads:
        copy.wait()

    block = block_ref[0]
    root_core = lax.rem(block, 2)
    is_root = lax.div(block, 2) == z

    def masked(k):
        return mask.at[chip(k)]

    def fill(ks, copies):
        arrive(copies)
        for k in ks:
            i = 2 * chip(k) + q
            mine = jnp.where(root_core == 0, x2[0, i], x2[1, i])
            mask[chip(k)] = jnp.where(is_root, mine, 0.0)

    fill(order[:3], wanted[0])
    phase[0] = 1
    far = [scatter_far(masked, 0, h) for h in range(2)]
    greet(0)
    fill(order[3:], wanted[1])
    last = [new(), new()]
    for h in range(2):
        scatter_near(masked, 0, h, last[h])
    others = to_twin(order, q)
    for h in range(2):
        scatter_mid(masked, 0, h, far[h], last[h])

    greet(1)

    phase[0] = 2
    halo = new()

    def lend(first, planes, to, shift):
        src, dst = act.at[pl.ds(first, planes)], act.at[pl.ds(first + shift, planes)]
        remote(src, dst, side(to), halo)

    act[pl.ds(HALO, 4)] = scatter_sum(masked, 0, 0, last[0])
    lend(HALO, 4, -1, NX)
    lend(HALO + 2, 2, 1, -NX)
    act[pl.ds(HALO + 4, 4)] = scatter_sum(masked, 0, 1, last[1])
    lend(HALO + 4, 2, -1, NX)
    lend(HALO + 4, 4, 1, -NX)

    r_high, r_low = split(rot[...])
    r_both = jnp.concatenate([r_high, r_low], 0)
    for j in range(0, NORB, 2):
        base = (j // 8) * 128
        shape = (128, 256)
        pick = indicator(
            shape, lambda r: r + base, lambda c: (j + (c >> 7)) * NB + (c & (NB - 1))
        )
        both = dot_nn(r_both[:, base : base + 128], jnp.where(pick, 1.0, 0.0).astype(BF))
        both = both[:NB] + both[NB:]
        own = indicator((NB, 256), lambda r: r & 7, lambda c: (c & 127) >> 4)
        both = jnp.where(own, both, 0.0).reshape(2, 8, 256).sum(1)
        packed[j] = both[:, :128]
        packed[j + 1] = both[:, 128:]
    panels[orb] = packed[orb]
    field = act[pl.ds(HALO, NX)]
    inner = (pot[...] - 1.5 * CENTER) * field
    for k in range(1, 7):
        near = (
            pltpu.roll(field, k, 1) + pltpu.roll(field, NY - k, 1)
            + pltpu.roll(field, k, 2) + pltpu.roll(field, NZ - k, 2)
        )
        inner = inner - (0.5 * SIDES[k - 1]) * near
    greet(2)
    arrive(others)
    for j in range(2):
        def cast(a, carry, j=j):
            high, low = split(x2[j, a])
            xh[j, a] = high
            xl[j, a] = low
            return carry
        lax.fori_loop(0, NB, cast, 0)
    greet(3)
    arrive(halo)
    for k in range(1, 7):
        inner = inner - (0.5 * SIDES[k - 1]) * (act[pl.ds(HALO + k, NX)] + act[pl.ds(HALO - k, NX)])
    amat[z] = inner

    cols = 2 * NB * NY

    def shard(k):
        return amat.at[chip(k)]

    def same_y(rows):
        return indicator((rows, cols), lambda r: r & (NY - 1), lambda c: c & (NY - 1))

    def x_pairs():
        for x in range(0, NX, 2):
            yield x, *(
                jnp.concatenate([r[:, :, x].reshape(cols, NZ), r[:, :, x + 1].reshape(cols, NZ)], 1)
                for r in (xh, xl)
            )

    def project(batch, ks):
        rows = len(ks) * NY
        gram = jnp.zeros((rows, cols), F32)
        for x, h_pair, l_pair in x_pairs():
            a_pair = jnp.concatenate([
                jnp.concatenate([shard(k)[x] for k in ks], 0),
                jnp.concatenate([shard(k)[x + 1] for k in ks], 0),
            ], 1)
            a_high, a_low = split(a_pair)
            both = dot_nt(jnp.concatenate([a_high, a_low], 0), h_pair)
            gram = gram + (both[:rows] + both[rows:] + dot_nt(a_high, l_pair))
        summed = jnp.where(same_y(rows), gram, 0.0).reshape(len(ks), NY, cols).sum(1)
        summed = jnp.concatenate([summed, jnp.zeros((4 - len(ks), cols), F32)], 0)
        of_orbital = indicator((cols, 128), lambda r: r >> 4, lambda c: c)
        s_both = jnp.concatenate(split(summed), 0)
        summed = dot_nn(s_both, jnp.where(of_orbital, 1.0, 0.0).astype(BF))
        pout[batch] = summed[:4] + summed[4:]
        sums = new(pbuf.at[batch])
        sent[7 + batch]["span"] = sums["span"]
        for k in range(NDOM):
            remote(pout.at[batch], pbuf.at[batch, dom], across(k), sums, sent[7 + batch])
        return sums

    def remove(batch, ks, copies, halves):
        rows = len(ks) * NY
        arrive(copies)
        proj = pbuf[batch].sum(0) * (1.0 / (NX * NDOM * NY * NZ))
        to_rows = indicator((128, cols), lambda r: r, lambda c: c >> 4)
        spread = dot_nn(
            jnp.concatenate(split(proj), 0), jnp.where(to_rows, 1.0, 0.0).astype(BF)
        )
        keep = same_y(rows)
        weights = []
        for first in (0, 4):
            one = spread[first : first + len(ks)]
            one = jnp.broadcast_to(one[:, None, :], (len(ks), NY, cols)).reshape(rows, cols)
            weights.append(jnp.where(keep, one, 0.0).astype(BF))
        k_both = jnp.concatenate(weights, 0)
        for x, h_pair, l_pair in x_pairs():
            both = dot_nn(k_both, h_pair)
            part = both[:rows] + both[rows:] + dot_nn(weights[0], l_pair)
            for i, k in enumerate(ks):
                remo[chip(k), x] = part[i * NY : (i + 1) * NY, :NZ]
                remo[chip(k), x + 1] = part[i * NY : (i + 1) * NY, NZ:]
            if x == 2 or x == 6:
                halves(x // 4)

    phase[0] = 3
    one, on = new(), new()
    gather_one(shard, 0, one)
    gather_one(shard, 1, one)
    two = [gather_two(shard, 0), gather_two(shard, 1)]
    arrive(one)
    batches = ((0, 1, -1), (2, -2), (3, -3, 4))
    sums = [project(0, batches[0])]
    gather_on(shard, 0, two[0], on, on)
    gather_on(shard, 1, two[1], on, on)
    sums.append(project(1, batches[1]))

    def removed(k):
        return remo.at[chip(k + 4)]

    def owned(k):
        return grad.at[2 * chip(k + 4) + 1 - q]

    phase[0] = 4
    far, last, twins = [], [new(), new()], [new(), new()]
    remove(0, batches[0], sums[0], lambda h: far.append(scatter_far(removed, 1, h)))
    arrive(on)
    base = new()
    remote(shard(4), ham, sibling, base)
    sums.append(project(2, batches[2]))
    panel_copies = new(panels.at[pl.ds(0, NORB - 1)])
    sent[6]["span"] = panel_copies["span"]
    for k in range(1, NORB):
        to = lax.rem(orb + k, NORB)
        remote(packed.at[to], panels.at[orb], (dom, to), panel_copies, sent[6])
    remove(1, batches[1], sums[1], lambda h: None)
    for h in range(2):
        scatter_mid(removed, 1, h, far[h], last[h])
    remove(2, batches[2], sums[2], lambda h: scatter_near(removed, 1, h, last[h]))

    phase[0] = 5

    def to_sibling(k, h):
        ref = owned(k).at[pl.ds(4 * h, 4)]
        remote(ref, ref, sibling, twins[h])

    arrive(base)
    two, one, three, four = [], [new(), new()], [new(), new()], [new(), new()]
    for h in range(2):
        half = pl.ds(4 * h, 4)
        owned(0)[half] = ham[half] - scatter_sum(removed, 1, h, last[h])
        two.append(gather_two(owned, h))
        gather_one(owned, h, one[h])
        to_sibling(0, h)

    arrive(panel_copies)
    rows = NB * NY
    panel = panels[owner_ref[0]]
    panel = jnp.broadcast_to(panel[:, None, :], (2, 8, 128)).reshape(NB, 128)
    own = indicator((NB, 128), lambda r: r & 7, lambda c: c >> 4)
    p_both = jnp.concatenate(split(jnp.where(own, panel, 0.0)), 0)
    of_column = indicator((rows, 128), lambda r: r >> 4, lambda c: c & (NB - 1))
    by_row = dot_nt(jnp.where(of_column, 1.0, 0.0).astype(BF), p_both).astype(BF)
    to_rows = indicator((NB, rows), lambda r: r, lambda c: c >> 4)
    to_rows = jnp.where(to_rows, 1.0, 0.0).astype(BF)
    keep = indicator((rows, rows), lambda r: r & (NY - 1), lambda c: c & (NY - 1))
    w_high, w_low = (
        jnp.where(keep, dot_nn(one_of, to_rows), 0.0).astype(BF)
        for one_of in (by_row[:, :NB], by_row[:, NB:])
    )
    w_both = jnp.concatenate([w_high, w_low], 0)

    w_ref[...] = w_both
    upd[:, 4:] = x2[q, :, 4:]

    for h in range(2):
        gather_on(owned, h, two[h], three[h], four[h], to_sibling)
    for h in range(2):
        arrive(one[h])
        to_sibling(-1, h)
        to_sibling(1, h)
    for h in range(2):
        arrive(three[h])
        to_sibling(-3, h)
        to_sibling(3, h)
        arrive(four[h])
        to_sibling(4, h)

    arrive(twins[0])
    for x in range(0, 4, 2):
        update(grad, w_both, x2.at[q], upd, x, x)
    arrive(twins[1])
    for group in sent:
        span(group).wait_send()
    assert next(groups) == recv.shape[0]


def update(grad, w_both, old, new, x, at):
    rows = NB * NY
    g_pair = jnp.concatenate([grad[:, x].reshape(rows, NZ), grad[:, x + 1].reshape(rows, NZ)], 1)
    g_high, g_low = split(g_pair)
    both = dot_nn(w_both, g_high)
    part = both[:rows] + both[rows:] + dot_nn(w_both[:rows], g_low)
    new[:, at] = old[:, x] + part[:, :NZ].reshape(NB, NY, NZ)
    new[:, at + 1] = old[:, x + 1] + part[:, NZ:].reshape(NB, NY, NZ)


def update_kernel(grad, w_ref, upd, grad_hbm, upd_hbm, done, sem):
    outs = []

    def out(src, dst):
        outs.append(pltpu.make_async_copy(src, dst, sem.at[len(outs)]))
        outs[-1].start()

    out(upd.at[:, pl.ds(0, 4)], upd_hbm.at[:, pl.ds(0, 4)])
    out(grad, grad_hbm)
    w_both = w_ref[...]
    for x in range(4, NX, 2):
        pair = pl.ds(x, 2)
        update(grad, w_both, upd, done, x, x - 4)
        out(done.at[:, pl.ds(x - 4, 2)], upd_hbm.at[:, pair])
    for copy in outs:
        copy.wait()


def per_device(orbitals, potential, rotation, block, owner):
    shard = (NX, NY, NZ)
    scratch = [
        pltpu.VMEM((2, NB, *shard), F32),
        pltpu.VMEM((2, NB, *shard), BF),
        pltpu.VMEM((2, NB, *shard), BF),
        pltpu.VMEM(shard, F32),
        pltpu.VMEM((NB, NB * NORB), F32),
        pltpu.VMEM((NCHIP, *shard), F32),
        pltpu.VMEM((NCHIP, *shard), F32),
        pltpu.VMEM((NX + 2 * HALO, NY, NZ), F32),
        pltpu.VMEM(shard, F32),
        pltpu.VMEM((NCHIP, *shard), F32),
        pltpu.VMEM((3, 4, 128), F32),
        pltpu.VMEM((3, NDOM, 4, 128), F32),
        pltpu.VMEM((NORB, 2, 128), F32),
        pltpu.VMEM((NORB, 2, 128), F32),
        pltpu.VMEM((2, 2, *shard), F32),
        pltpu.VMEM((2, 2, *shard), F32),
        pltpu.VMEM((2, 2, *shard), F32),
        pltpu.VMEM((2, 2, *shard), F32),
        pltpu.VMEM((2, 2, *shard), F32),
        pltpu.SemaphoreType.DMA((10,)),
        pltpu.SemaphoreType.DMA((39,)),
        pltpu.SemaphoreType.DMA((3,)),
        pltpu.SemaphoreType.REGULAR((3,)),
    ]
    hbm = pl.BlockSpec(memory_space=pl.ANY)
    smem = pl.BlockSpec(memory_space=pltpu.SMEM)
    vmem = pl.BlockSpec(memory_space=pltpu.VMEM)
    whole = jax.ShapeDtypeStruct((NB, *shard), F32)
    arrays = (pltpu.with_memory_space_constraint(v, pltpu.HBM) for v in (orbitals, potential, rotation))
    gradient, weights, updated = pl.pallas_call(
        kernel,
        out_shape=(whole, jax.ShapeDtypeStruct((2 * NB * NY, NB * NY), BF), whole),
        in_specs=[smem, smem, hbm, hbm, hbm],
        out_specs=(vmem, vmem, vmem),
        scratch_shapes=scratch,
        compiler_params=pltpu.CompilerParams(
            collective_id=0, has_side_effects=True, vmem_limit_bytes=40 << 20
        ),
        cost_estimate=pl.CostEstimate(flops=1 << 28, bytes_accessed=3 << 20, transcendentals=0),
        name="gradient",
    )(block, owner, *arrays)
    return pl.pallas_call(
        update_kernel,
        out_shape=(whole, whole),
        in_specs=[vmem, vmem, vmem],
        out_specs=(hbm, hbm),
        scratch_shapes=[
            pltpu.VMEM((NB, NX // 2, NY, NZ), F32),
            pltpu.SemaphoreType.DMA((4,)),
        ],
        compiler_params=pltpu.CompilerParams(vmem_limit_bytes=16 << 20),
        cost_estimate=pl.CostEstimate(flops=1 << 28, bytes_accessed=4 << 20, transcendentals=0),
        name="update",
    )(gradient, weights, updated)


def solution(mesh):
    in_specs = (P("orb", "dom", None, None), P("dom", None, None), P("orb", None), P(), P())
    out_specs = (P(None, "dom", None, None), P("orb", "dom", None, None))
    return jax.shard_map(
        per_device, mesh=mesh, in_specs=in_specs, out_specs=out_specs, check_vma=False
    )
```

```python
import itertools
import math

import jax
import jax.numpy as jnp
from jax import lax
from jax.experimental import pallas as pl
from jax.experimental.pallas import tpu as pltpu
from jax.sharding import PartitionSpec as P

CENTER = -5369.0 / 1800.0
SIDES = (12.0 / 7.0, -15.0 / 56.0, 10.0 / 189.0, -1.0 / 112.0, 2.0 / 1925.0, -1.0 / 16632.0)

MESH = pl.DeviceIdType.MESH
NB = 16
NX, NY, NZ = 8, 16, 128
NDOM, NORB, NCHIP = 16, 16, 8
HALO = 6
BF = jnp.bfloat16
F32 = jnp.float32


def split(value):
    high = value.astype(BF)
    return high, (value - high.astype(F32)).astype(BF)


def dot_nt(a, b):
    return lax.dot_general(a, b, (((1,), (1,)), ((), ())), preferred_element_type=F32)


def dot_nn(a, b):
    return lax.dot_general(a, b, (((1,), (0,)), ((), ())), preferred_element_type=F32)


def indicator(shape, row_of, col_of):
    rows = lax.broadcasted_iota(jnp.int32, shape, 0)
    cols = lax.broadcasted_iota(jnp.int32, shape, 1)
    return row_of(rows) == col_of(cols)


def kernel(
    block_ref, owner_ref, x_hbm, pot_hbm, rot_hbm, grad, w_ref, upd,
    x2, xh, xl, pot, rot, mask, remo, act, ham, amat, pout, pbuf, packed, panels,
    a1, a2, d1, b2, sb, send, recv, loc, greetings,
):
    dom = lax.axis_index("dom")
    orb = lax.axis_index("orb")
    z = lax.div(orb, 2)
    q = lax.rem(orb, 2)

    def chip(k):
        return lax.rem(z + (k + 2 * NCHIP), NCHIP)

    def peer(k):
        return (dom, 2 * chip(k) + q)

    def side(k):
        return (lax.rem(dom + (k + NDOM), NDOM), orb)

    twin = orb + 1 - 2 * q
    sibling = (dom, twin)

    def across(k):
        return (lax.rem(dom + k, NDOM), twin)
    groups = itertools.count()
    sent = [dict(sem=i, rows=0) for i in range(send.shape[0])]
    phase = [0]

    def new(span=None):
        return dict(sem=next(groups), rows=0, span=span)

    def remote(src, dst, device, group, sends=None):
        sends = sent[phase[0]] if sends is None else sends
        pltpu.make_async_remote_copy(
            src_ref=src, dst_ref=dst, send_sem=send.at[sends["sem"]], recv_sem=recv.at[group["sem"]],
            device_id=device, device_id_type=MESH,
        ).start()
        for one in (group, sends):
            one["rows"] += math.prod(src.shape[:-1])

    def span(group):
        planes = group["rows"] // NY
        if group.get("span") is not None:
            ref = group["span"]
        elif planes <= act.shape[0]:
            ref = act.at[pl.ds(0, planes)]
        else:
            ref = x2.at[0, pl.ds(0, planes // NX)]
        assert math.prod(ref.shape[:-1]) == group["rows"]
        return pltpu.make_async_remote_copy(
            src_ref=ref, dst_ref=ref, send_sem=send.at[group["sem"] % len(sent)],
            recv_sem=recv.at[group["sem"]], device_id=sibling, device_id_type=MESH,
        )

    def arrive(*waited):
        for group in waited:
            span(group).wait_recv()

    loads = [
        pltpu.make_async_copy(src, dst, loc.at[i])
        for i, (src, dst) in enumerate(((x_hbm, x2.at[q]), (pot_hbm, pot), (rot_hbm, rot)))
    ]
    loads[0].start()
    row, col = lax.div(dom, 4), lax.rem(dom, 4)
    around = [
        (4 * lax.rem(row + i, 4) + lax.rem(col + j, 4), orb) for i, j in ((0, 1), (0, 3), (1, 0), (3, 0))
    ]
    near = [peer(2), peer(-2), peer(1), peer(-1), sibling, side(1), side(-1), *around]
    barrier = pltpu.get_barrier_semaphore()
    for device in near:
        pl.semaphore_signal(barrier, inc=1, device_id=device, device_id_type=MESH)
    for copy in loads[1:]:
        copy.start()
    pl.semaphore_wait(barrier, len(near))

    def greet(i):
        if i > 0:
            pl.semaphore_wait(greetings.at[i - 1], len(around))
        if i < 3:
            for device in around:
                pl.semaphore_signal(greetings.at[i], inc=1, device_id=device, device_id_type=MESH)

    def scatter_far(part, slot, h):
        whole, front, back = pl.ds(4 * h, 4), pl.ds(4 * h, 2), pl.ds(4 * h + 2, 2)
        up, down = new(), new()
        remote(part(4).at[front], a2.at[slot, 0, front], peer(2), up)
        remote(part(4).at[back], a2.at[slot, 1, back], peer(-2), down)
        remote(part(3).at[whole], a1.at[slot, 0, whole], peer(1), up)
        remote(part(-3).at[whole], a1.at[slot, 1, whole], peer(-1), down)
        return up, down

    def scatter_mid(part, slot, h, far, last):
        whole, front, back = pl.ds(4 * h, 4), pl.ds(4 * h, 2), pl.ds(4 * h + 2, 2)
        for i, sign, quarter in ((0, 1, front), (1, -1, back)):
            arrive(far[i])
            sb[slot, i, whole] = part(2 * sign)[whole] + a1[slot, i, whole]
            sb[slot, i, quarter] = sb[slot, i, quarter] + a2[slot, i, quarter]
            remote(sb.at[slot, i, whole], b2.at[slot, i, whole], peer(2 * sign), last)

    def scatter_near(part, slot, h, last):
        whole = pl.ds(4 * h, 4)
        remote(part(1).at[whole], d1.at[slot, 0, whole], peer(1), last)
        remote(part(-1).at[whole], d1.at[slot, 1, whole], peer(-1), last)

    def scatter_sum(part, slot, h, last):
        whole = pl.ds(4 * h, 4)
        arrive(last)
        return (
            part(0)[whole]
            + (d1[slot, 0, whole] + d1[slot, 1, whole])
            + (b2[slot, 0, whole] + b2[slot, 1, whole])
        )

    def give(shard, k, to, planes, group):
        ref = shard(k).at[planes]
        remote(ref, ref, peer(to), group)

    def gather_two(shard, h):
        whole = pl.ds(4 * h, 4)
        two = new(), new()
        give(shard, 0, 2, whole, two[0])
        give(shard, 0, -2, whole, two[1])
        return two

    def gather_one(shard, h, group):
        whole = pl.ds(4 * h, 4)
        give(shard, 0, 1, whole, group)
        give(shard, 0, -1, whole, group)

    def gather_on(shard, h, two, three, four, arrived=lambda k, h: None):
        whole, front, back = pl.ds(4 * h, 4), pl.ds(4 * h, 2), pl.ds(4 * h + 2, 2)
        arrive(two[0])
        give(shard, -2, 2, front, four)
        give(shard, -2, 1, whole, three)
        arrived(-2, h)
        arrive(two[1])
        give(shard, 2, -2, back, four)
        give(shard, 2, -1, whole, three)
        arrived(2, h)

    order = (4, 3, -3, 2, -2, 1, -1, 0)

    def to_twin(ks, parity):
        group = new()
        for k in ks:
            i = 2 * chip(k) + parity
            remote(x_hbm.at[i], x2.at[q, i], sibling, group)
        return group

    wanted = to_twin(order[:3], 1 - q), to_twin(order[3:], 1 - q)

    for copy in loads:
        copy.wait()

    block = block_ref[0]
    root_core = lax.rem(block, 2)
    is_root = lax.div(block, 2) == z

    def masked(k):
        return mask.at[chip(k)]

    def fill(ks, copies):
        arrive(copies)
        for k in ks:
            i = 2 * chip(k) + q
            mine = jnp.where(root_core == 0, x2[0, i], x2[1, i])
            mask[chip(k)] = jnp.where(is_root, mine, 0.0)

    fill(order[:3], wanted[0])
    phase[0] = 1
    far = [scatter_far(masked, 0, h) for h in range(2)]
    greet(0)
    fill(order[3:], wanted[1])
    last = [new(), new()]
    for h in range(2):
        scatter_near(masked, 0, h, last[h])
    others = to_twin(order, q)
    for h in range(2):
        scatter_mid(masked, 0, h, far[h], last[h])

    greet(1)

    phase[0] = 2
    halo = new()

    def lend(first, planes, to, shift):
        src, dst = act.at[pl.ds(first, planes)], act.at[pl.ds(first + shift, planes)]
        remote(src, dst, side(to), halo)

    act[pl.ds(HALO, 4)] = scatter_sum(masked, 0, 0, last[0])
    lend(HALO, 4, -1, NX)
    lend(HALO + 2, 2, 1, -NX)
    act[pl.ds(HALO + 4, 4)] = scatter_sum(masked, 0, 1, last[1])
    lend(HALO + 4, 2, -1, NX)
    lend(HALO + 4, 4, 1, -NX)

    r_high, r_low = split(rot[...])
    r_both = jnp.concatenate([r_high, r_low], 0)
    for j in range(0, NORB, 2):
        base = (j // 8) * 128
        shape = (128, 256)
        pick = indicator(
            shape, lambda r: r + base, lambda c: (j + (c >> 7)) * NB + (c & (NB - 1))
        )
        both = dot_nn(r_both[:, base : base + 128], jnp.where(pick, 1.0, 0.0).astype(BF))
        both = both[:NB] + both[NB:]
        own = indicator((NB, 256), lambda r: r & 7, lambda c: (c & 127) >> 4)
        both = jnp.where(own, both, 0.0).reshape(2, 8, 256).sum(1)
        packed[j] = both[:, :128]
        packed[j + 1] = both[:, 128:]
    panels[orb] = packed[orb]
    field = act[pl.ds(HALO, NX)]
    inner = (pot[...] - 1.5 * CENTER) * field
    for k in range(1, 7):
        near = (
            pltpu.roll(field, k, 1) + pltpu.roll(field, NY - k, 1)
            + pltpu.roll(field, k, 2) + pltpu.roll(field, NZ - k, 2)
        )
        inner = inner - (0.5 * SIDES[k - 1]) * near
    greet(2)
    arrive(others)
    for j in range(2):
        def cast(a, carry, j=j):
            high, low = split(x2[j, a])
            xh[j, a] = high
            xl[j, a] = low
            return carry
        lax.fori_loop(0, NB, cast, 0)
    greet(3)
    arrive(halo)
    for k in range(1, 7):
        inner = inner - (0.5 * SIDES[k - 1]) * (act[pl.ds(HALO + k, NX)] + act[pl.ds(HALO - k, NX)])
    amat[z] = inner

    cols = 2 * NB * NY

    def shard(k):
        return amat.at[chip(k)]

    def same_y(rows):
        return indicator((rows, cols), lambda r: r & (NY - 1), lambda c: c & (NY - 1))

    def x_pairs():
        for x in range(0, NX, 2):
            yield x, *(
                jnp.concatenate([r[:, :, x].reshape(cols, NZ), r[:, :, x + 1].reshape(cols, NZ)], 1)
                for r in (xh, xl)
            )

    def project(batch, ks):
        rows = len(ks) * NY
        gram = jnp.zeros((rows, cols), F32)
        for x, h_pair, l_pair in x_pairs():
            a_pair = jnp.concatenate([
                jnp.concatenate([shard(k)[x] for k in ks], 0),
                jnp.concatenate([shard(k)[x + 1] for k in ks], 0),
            ], 1)
            a_high, a_low = split(a_pair)
            both = dot_nt(jnp.concatenate([a_high, a_low], 0), h_pair)
            gram = gram + (both[:rows] + both[rows:] + dot_nt(a_high, l_pair))
        summed = jnp.where(same_y(rows), gram, 0.0).reshape(len(ks), NY, cols).sum(1)
        summed = jnp.concatenate([summed, jnp.zeros((4 - len(ks), cols), F32)], 0)
        of_orbital = indicator((cols, 128), lambda r: r >> 4, lambda c: c)
        s_both = jnp.concatenate(split(summed), 0)
        summed = dot_nn(s_both, jnp.where(of_orbital, 1.0, 0.0).astype(BF))
        pout[batch] = summed[:4] + summed[4:]
        sums = new(pbuf.at[batch])
        sent[7 + batch]["span"] = sums["span"]
        for k in range(NDOM):
            remote(pout.at[batch], pbuf.at[batch, dom], across(k), sums, sent[7 + batch])
        return sums

    def remove(batch, ks, copies, halves):
        rows = len(ks) * NY
        arrive(copies)
        proj = pbuf[batch].sum(0) * (1.0 / (NX * NDOM * NY * NZ))
        to_rows = indicator((128, cols), lambda r: r, lambda c: c >> 4)
        spread = dot_nn(
            jnp.concatenate(split(proj), 0), jnp.where(to_rows, 1.0, 0.0).astype(BF)
        )
        keep = same_y(rows)
        weights = []
        for first in (0, 4):
            one = spread[first : first + len(ks)]
            one = jnp.broadcast_to(one[:, None, :], (len(ks), NY, cols)).reshape(rows, cols)
            weights.append(jnp.where(keep, one, 0.0).astype(BF))
        k_both = jnp.concatenate(weights, 0)
        for x, h_pair, l_pair in x_pairs():
            both = dot_nn(k_both, h_pair)
            part = both[:rows] + both[rows:] + dot_nn(weights[0], l_pair)
            for i, k in enumerate(ks):
                remo[chip(k), x] = part[i * NY : (i + 1) * NY, :NZ]
                remo[chip(k), x + 1] = part[i * NY : (i + 1) * NY, NZ:]
            if x == 2 or x == 6:
                halves(x // 4)

    phase[0] = 3
    one, on = new(), new()
    gather_one(shard, 0, one)
    gather_one(shard, 1, one)
    two = [gather_two(shard, 0), gather_two(shard, 1)]
    arrive(one)
    batches = ((0, 1, -1), (2, -2), (3, -3, 4))
    sums = [project(0, batches[0])]
    gather_on(shard, 0, two[0], on, on)
    gather_on(shard, 1, two[1], on, on)
    sums.append(project(1, batches[1]))

    def removed(k):
        return remo.at[chip(k + 4)]

    def owned(k):
        return grad.at[2 * chip(k + 4) + 1 - q]

    phase[0] = 4
    far, last, twins = [], [new(), new()], [new(), new()]
    remove(0, batches[0], sums[0], lambda h: far.append(scatter_far(removed, 1, h)))
    arrive(on)
    base = new()
    remote(shard(4), ham, sibling, base)
    sums.append(project(2, batches[2]))
    remove(1, batches[1], sums[1], lambda h: None)
    for h in range(2):
        scatter_mid(removed, 1, h, far[h], last[h])
    panel_copies = new(panels.at[pl.ds(0, NORB - 1)])
    sent[6]["span"] = panel_copies["span"]
    for k in range(1, NORB):
        to = lax.rem(orb + k, NORB)
        remote(packed.at[to], panels.at[orb], (dom, to), panel_copies, sent[6])
    remove(2, batches[2], sums[2], lambda h: scatter_near(removed, 1, h, last[h]))

    phase[0] = 5

    def to_sibling(k, h):
        ref = owned(k).at[pl.ds(4 * h, 4)]
        remote(ref, ref, sibling, twins[h])

    arrive(base)
    two, one, three, four = [], [new(), new()], [new(), new()], [new(), new()]
    for h in range(2):
        half = pl.ds(4 * h, 4)
        owned(0)[half] = ham[half] - scatter_sum(removed, 1, h, last[h])
        two.append(gather_two(owned, h))
        gather_one(owned, h, one[h])
        to_sibling(0, h)

    arrive(panel_copies)
    rows = NB * NY
    panel = panels[owner_ref[0]]
    panel = jnp.broadcast_to(panel[:, None, :], (2, 8, 128)).reshape(NB, 128)
    own = indicator((NB, 128), lambda r: r & 7, lambda c: c >> 4)
    p_both = jnp.concatenate(split(jnp.where(own, panel, 0.0)), 0)
    of_column = indicator((rows, 128), lambda r: r >> 4, lambda c: c & (NB - 1))
    by_row = dot_nt(jnp.where(of_column, 1.0, 0.0).astype(BF), p_both).astype(BF)
    to_rows = indicator((NB, rows), lambda r: r, lambda c: c >> 4)
    to_rows = jnp.where(to_rows, 1.0, 0.0).astype(BF)
    keep = indicator((rows, rows), lambda r: r & (NY - 1), lambda c: c & (NY - 1))
    w_high, w_low = (
        jnp.where(keep, dot_nn(one_of, to_rows), 0.0).astype(BF)
        for one_of in (by_row[:, :NB], by_row[:, NB:])
    )
    w_both = jnp.concatenate([w_high, w_low], 0)

    w_ref[...] = w_both
    upd[:, 4:] = x2[q, :, 4:]

    for h in range(2):
        gather_on(owned, h, two[h], three[h], four[h], to_sibling)
    for h in range(2):
        arrive(one[h])
        to_sibling(-1, h)
        to_sibling(1, h)
    for h in range(2):
        arrive(three[h])
        to_sibling(-3, h)
        to_sibling(3, h)
        arrive(four[h])
        to_sibling(4, h)

    arrive(twins[0])
    for x in range(0, 4, 2):
        update(grad, w_both, x2.at[q], upd, x, x)
    arrive(twins[1])
    for group in sent:
        span(group).wait_send()
    assert next(groups) == recv.shape[0]


def update(grad, w_both, old, new, x, at):
    rows = NB * NY
    g_pair = jnp.concatenate([grad[:, x].reshape(rows, NZ), grad[:, x + 1].reshape(rows, NZ)], 1)
    g_high, g_low = split(g_pair)
    both = dot_nn(w_both, g_high)
    part = both[:rows] + both[rows:] + dot_nn(w_both[:rows], g_low)
    new[:, at] = old[:, x] + part[:, :NZ].reshape(NB, NY, NZ)
    new[:, at + 1] = old[:, x + 1] + part[:, NZ:].reshape(NB, NY, NZ)


def update_kernel(grad, w_ref, upd, grad_hbm, upd_hbm, done, sem):
    outs = []

    def out(src, dst):
        outs.append(pltpu.make_async_copy(src, dst, sem.at[len(outs)]))
        outs[-1].start()

    out(upd.at[:, pl.ds(0, 4)], upd_hbm.at[:, pl.ds(0, 4)])
    out(grad, grad_hbm)
    w_both = w_ref[...]
    for x in range(4, NX, 2):
        pair = pl.ds(x, 2)
        update(grad, w_both, upd, done, x, x - 4)
        out(done.at[:, pl.ds(x - 4, 2)], upd_hbm.at[:, pair])
    for copy in outs:
        copy.wait()


def per_device(orbitals, potential, rotation, block, owner):
    shard = (NX, NY, NZ)
    scratch = [
        pltpu.VMEM((2, NB, *shard), F32),
        pltpu.VMEM((2, NB, *shard), BF),
        pltpu.VMEM((2, NB, *shard), BF),
        pltpu.VMEM(shard, F32),
        pltpu.VMEM((NB, NB * NORB), F32),
        pltpu.VMEM((NCHIP, *shard), F32),
        pltpu.VMEM((NCHIP, *shard), F32),
        pltpu.VMEM((NX + 2 * HALO, NY, NZ), F32),
        pltpu.VMEM(shard, F32),
        pltpu.VMEM((NCHIP, *shard), F32),
        pltpu.VMEM((3, 4, 128), F32),
        pltpu.VMEM((3, NDOM, 4, 128), F32),
        pltpu.VMEM((NORB, 2, 128), F32),
        pltpu.VMEM((NORB, 2, 128), F32),
        pltpu.VMEM((2, 2, *shard), F32),
        pltpu.VMEM((2, 2, *shard), F32),
        pltpu.VMEM((2, 2, *shard), F32),
        pltpu.VMEM((2, 2, *shard), F32),
        pltpu.VMEM((2, 2, *shard), F32),
        pltpu.SemaphoreType.DMA((10,)),
        pltpu.SemaphoreType.DMA((39,)),
        pltpu.SemaphoreType.DMA((3,)),
        pltpu.SemaphoreType.REGULAR((3,)),
    ]
    hbm = pl.BlockSpec(memory_space=pl.ANY)
    smem = pl.BlockSpec(memory_space=pltpu.SMEM)
    vmem = pl.BlockSpec(memory_space=pltpu.VMEM)
    whole = jax.ShapeDtypeStruct((NB, *shard), F32)
    arrays = (pltpu.with_memory_space_constraint(v, pltpu.HBM) for v in (orbitals, potential, rotation))
    gradient, weights, updated = pl.pallas_call(
        kernel,
        out_shape=(whole, jax.ShapeDtypeStruct((2 * NB * NY, NB * NY), BF), whole),
        in_specs=[smem, smem, hbm, hbm, hbm],
        out_specs=(vmem, vmem, vmem),
        scratch_shapes=scratch,
        compiler_params=pltpu.CompilerParams(
            collective_id=0, has_side_effects=True, vmem_limit_bytes=40 << 20
        ),
        cost_estimate=pl.CostEstimate(flops=1 << 28, bytes_accessed=3 << 20, transcendentals=0),
        name="gradient",
    )(block, owner, *arrays)
    return pl.pallas_call(
        update_kernel,
        out_shape=(whole, whole),
        in_specs=[vmem, vmem, vmem],
        out_specs=(hbm, hbm),
        scratch_shapes=[
            pltpu.VMEM((NB, NX // 2, NY, NZ), F32),
            pltpu.SemaphoreType.DMA((4,)),
        ],
        compiler_params=pltpu.CompilerParams(vmem_limit_bytes=16 << 20),
        cost_estimate=pl.CostEstimate(flops=1 << 28, bytes_accessed=4 << 20, transcendentals=0),
        name="update",
    )(gradient, weights, updated)


def solution(mesh):
    in_specs = (P("orb", "dom", None, None), P("dom", None, None), P("orb", None), P(), P())
    out_specs = (P(None, "dom", None, None), P("orb", "dom", None, None))
    return jax.shard_map(
        per_device, mesh=mesh, in_specs=in_specs, out_specs=out_specs, check_vma=False
    )
```

```python
import itertools
import math

import jax
import jax.numpy as jnp
from jax import lax
from jax.experimental import pallas as pl
from jax.experimental.pallas import tpu as pltpu
from jax.sharding import PartitionSpec as P

CENTER = -5369.0 / 1800.0
SIDES = (12.0 / 7.0, -15.0 / 56.0, 10.0 / 189.0, -1.0 / 112.0, 2.0 / 1925.0, -1.0 / 16632.0)

MESH = pl.DeviceIdType.MESH
NB = 16
NX, NY, NZ = 8, 16, 128
NDOM, NORB, NCHIP = 16, 16, 8
HALO = 6
BF = jnp.bfloat16
F32 = jnp.float32


def split(value):
    high = value.astype(BF)
    return high, (value - high.astype(F32)).astype(BF)


def dot_nt(a, b):
    return lax.dot_general(a, b, (((1,), (1,)), ((), ())), preferred_element_type=F32)


def dot_nn(a, b):
    return lax.dot_general(a, b, (((1,), (0,)), ((), ())), preferred_element_type=F32)


def indicator(shape, row_of, col_of):
    rows = lax.broadcasted_iota(jnp.int32, shape, 0)
    cols = lax.broadcasted_iota(jnp.int32, shape, 1)
    return row_of(rows) == col_of(cols)


def kernel(
    block_ref, owner_ref, x_hbm, pot_hbm, rot_hbm, grad, w_ref, upd,
    x2, xh, xl, pot, rot, mask, remo, act, ham, amat, pout, pbuf, keep, of_orbital, to_cells, packed, panels,
    a1, a2, d1, b2, sb, send, recv, loc, greetings,
):
    dom = lax.axis_index("dom")
    orb = lax.axis_index("orb")
    z = lax.div(orb, 2)
    q = lax.rem(orb, 2)

    def chip(k):
        return lax.rem(z + (k + 2 * NCHIP), NCHIP)

    def peer(k):
        return (dom, 2 * chip(k) + q)

    def side(k):
        return (lax.rem(dom + (k + NDOM), NDOM), orb)

    twin = orb + 1 - 2 * q
    sibling = (dom, twin)

    def across(k):
        return (lax.rem(dom + k, NDOM), twin)
    groups = itertools.count()
    sent = [dict(sem=i, rows=0) for i in range(send.shape[0])]
    phase = [0]

    def new(span=None):
        return dict(sem=next(groups), rows=0, span=span)

    def remote(src, dst, device, group, sends=None):
        sends = sent[phase[0]] if sends is None else sends
        pltpu.make_async_remote_copy(
            src_ref=src, dst_ref=dst, send_sem=send.at[sends["sem"]], recv_sem=recv.at[group["sem"]],
            device_id=device, device_id_type=MESH,
        ).start()
        for one in (group, sends):
            one["rows"] += math.prod(src.shape[:-1])

    def span(group):
        planes = group["rows"] // NY
        if group.get("span") is not None:
            ref = group["span"]
        elif planes <= act.shape[0]:
            ref = act.at[pl.ds(0, planes)]
        else:
            ref = x2.at[0, pl.ds(0, planes // NX)]
        assert math.prod(ref.shape[:-1]) == group["rows"]
        return pltpu.make_async_remote_copy(
            src_ref=ref, dst_ref=ref, send_sem=send.at[group["sem"] % len(sent)],
            recv_sem=recv.at[group["sem"]], device_id=sibling, device_id_type=MESH,
        )

    def arrive(*waited):
        for group in waited:
            span(group).wait_recv()

    loads = [
        pltpu.make_async_copy(src, dst, loc.at[i])
        for i, (src, dst) in enumerate(((x_hbm, x2.at[q]), (pot_hbm, pot), (rot_hbm, rot)))
    ]
    loads[0].start()
    row, col = lax.div(dom, 4), lax.rem(dom, 4)
    around = [
        (4 * lax.rem(row + i, 4) + lax.rem(col + j, 4), orb) for i, j in ((0, 1), (0, 3), (1, 0), (3, 0))
    ]
    near = [peer(2), peer(-2), peer(1), peer(-1), sibling, side(1), side(-1), *around]
    barrier = pltpu.get_barrier_semaphore()
    for device in near:
        pl.semaphore_signal(barrier, inc=1, device_id=device, device_id_type=MESH)
    for copy in loads[1:]:
        copy.start()
    pl.semaphore_wait(barrier, len(near))

    def greet(i):
        if i > 0:
            pl.semaphore_wait(greetings.at[i - 1], len(around))
        if i < 3:
            for device in around:
                pl.semaphore_signal(greetings.at[i], inc=1, device_id=device, device_id_type=MESH)

    def scatter_far(part, slot, h):
        whole, front, back = pl.ds(4 * h, 4), pl.ds(4 * h, 2), pl.ds(4 * h + 2, 2)
        up, down = new(), new()
        remote(part(4).at[front], a2.at[slot, 0, front], peer(2), up)
        remote(part(4).at[back], a2.at[slot, 1, back], peer(-2), down)
        remote(part(3).at[whole], a1.at[slot, 0, whole], peer(1), up)
        remote(part(-3).at[whole], a1.at[slot, 1, whole], peer(-1), down)
        return up, down

    def scatter_mid(part, slot, h, far, last):
        whole, front, back = pl.ds(4 * h, 4), pl.ds(4 * h, 2), pl.ds(4 * h + 2, 2)
        for i, sign, quarter in ((0, 1, front), (1, -1, back)):
            arrive(far[i])
            sb[slot, i, whole] = part(2 * sign)[whole] + a1[slot, i, whole]
            sb[slot, i, quarter] = sb[slot, i, quarter] + a2[slot, i, quarter]
            remote(sb.at[slot, i, whole], b2.at[slot, i, whole], peer(2 * sign), last)

    def scatter_near(part, slot, h, last):
        whole = pl.ds(4 * h, 4)
        remote(part(1).at[whole], d1.at[slot, 0, whole], peer(1), last)
        remote(part(-1).at[whole], d1.at[slot, 1, whole], peer(-1), last)

    def scatter_sum(part, slot, h, last):
        whole = pl.ds(4 * h, 4)
        arrive(last)
        return (
            part(0)[whole]
            + (d1[slot, 0, whole] + d1[slot, 1, whole])
            + (b2[slot, 0, whole] + b2[slot, 1, whole])
        )

    def give(shard, k, to, planes, group):
        ref = shard(k).at[planes]
        remote(ref, ref, peer(to), group)

    def gather_two(shard, h):
        whole = pl.ds(4 * h, 4)
        two = new(), new()
        give(shard, 0, 2, whole, two[0])
        give(shard, 0, -2, whole, two[1])
        return two

    def gather_one(shard, h, group):
        whole = pl.ds(4 * h, 4)
        give(shard, 0, 1, whole, group)
        give(shard, 0, -1, whole, group)

    def gather_on(shard, h, two, three, four, arrived=lambda k, h: None):
        whole, front, back = pl.ds(4 * h, 4), pl.ds(4 * h, 2), pl.ds(4 * h + 2, 2)
        arrive(two[0])
        give(shard, -2, 2, front, four)
        give(shard, -2, 1, whole, three)
        arrived(-2, h)
        arrive(two[1])
        give(shard, 2, -2, back, four)
        give(shard, 2, -1, whole, three)
        arrived(2, h)

    order = (4, 3, -3, 2, -2, 1, -1, 0)

    def to_twin(ks, parity):
        group = new()
        for k in ks:
            i = 2 * chip(k) + parity
            remote(x_hbm.at[i], x2.at[q, i], sibling, group)
        return group

    wanted = to_twin(order[:3], 1 - q), to_twin(order[3:], 1 - q)

    for copy in loads:
        copy.wait()

    block = block_ref[0]
    root_core = lax.rem(block, 2)
    is_root = lax.div(block, 2) == z

    def masked(k):
        return mask.at[chip(k)]

    def fill(ks, copies):
        arrive(copies)
        for k in ks:
            i = 2 * chip(k) + q
            mine = jnp.where(root_core == 0, x2[0, i], x2[1, i])
            mask[chip(k)] = jnp.where(is_root, mine, 0.0)

    fill(order[:3], wanted[0])
    phase[0] = 1
    far = [scatter_far(masked, 0, h) for h in range(2)]
    greet(0)
    fill(order[3:], wanted[1])
    last = [new(), new()]
    for h in range(2):
        scatter_near(masked, 0, h, last[h])
    others = to_twin(order, q)
    for h in range(2):
        scatter_mid(masked, 0, h, far[h], last[h])

    greet(1)

    phase[0] = 2
    halo = new()

    def lend(first, planes, to, shift):
        src, dst = act.at[pl.ds(first, planes)], act.at[pl.ds(first + shift, planes)]
        remote(src, dst, side(to), halo)

    act[pl.ds(HALO, 4)] = scatter_sum(masked, 0, 0, last[0])
    lend(HALO, 4, -1, NX)
    lend(HALO + 2, 2, 1, -NX)
    act[pl.ds(HALO + 4, 4)] = scatter_sum(masked, 0, 1, last[1])
    lend(HALO + 4, 2, -1, NX)
    lend(HALO + 4, 4, 1, -NX)

    r_high, r_low = split(rot[...])
    r_both = jnp.concatenate([r_high, r_low], 0)
    for j in range(0, NORB, 2):
        base = (j // 8) * 128
        shape = (128, 256)
        pick = indicator(
            shape, lambda r: r + base, lambda c: (j + (c >> 7)) * NB + (c & (NB - 1))
        )
        both = dot_nn(r_both[:, base : base + 128], jnp.where(pick, 1.0, 0.0).astype(BF))
        both = both[:NB] + both[NB:]
        own = indicator((NB, 256), lambda r: r & 7, lambda c: (c & 127) >> 4)
        both = jnp.where(own, both, 0.0).reshape(2, 8, 256).sum(1)
        packed[j] = both[:, :128]
        packed[j + 1] = both[:, 128:]
    panels[orb] = packed[orb]
    cols = 2 * NB * NY
    same_y = indicator((3 * NY, cols), lambda r: r & (NY - 1), lambda c: c & (NY - 1))
    keep[...] = jnp.where(same_y, 1.0, 0.0)
    pick = indicator((cols, 128), lambda r: r >> 4, lambda c: c)
    of_orbital[...] = jnp.where(pick, 1.0, 0.0).astype(BF)
    pick = indicator((128, cols), lambda r: r, lambda c: c >> 4)
    to_cells[...] = jnp.where(pick, 1.0, 0.0).astype(BF)

    field = act[pl.ds(HALO, NX)]
    inner = (pot[...] - 1.5 * CENTER) * field
    for k in range(1, 7):
        near = (
            pltpu.roll(field, k, 1) + pltpu.roll(field, NY - k, 1)
            + pltpu.roll(field, k, 2) + pltpu.roll(field, NZ - k, 2)
        )
        inner = inner - (0.5 * SIDES[k - 1]) * near
    greet(2)
    arrive(others)
    for j in range(2):
        def cast(a, carry, j=j):
            high, low = split(x2[j, a])
            xh[j, a] = high
            xl[j, a] = low
            return carry
        lax.fori_loop(0, NB, cast, 0)
    greet(3)
    arrive(halo)
    for k in range(1, 7):
        inner = inner - (0.5 * SIDES[k - 1]) * (act[pl.ds(HALO + k, NX)] + act[pl.ds(HALO - k, NX)])
    amat[z] = inner

    def shard(k):
        return amat.at[chip(k)]

    def x_pairs():
        for x in range(0, NX, 2):
            yield x, *(
                jnp.concatenate([r[:, :, x].reshape(cols, NZ), r[:, :, x + 1].reshape(cols, NZ)], 1)
                for r in (xh, xl)
            )

    def project(batch, ks):
        rows = len(ks) * NY
        gram = jnp.zeros((rows, cols), F32)
        for x, h_pair, l_pair in x_pairs():
            a_pair = jnp.concatenate([
                jnp.concatenate([shard(k)[x] for k in ks], 0),
                jnp.concatenate([shard(k)[x + 1] for k in ks], 0),
            ], 1)
            a_high, a_low = split(a_pair)
            both = dot_nt(jnp.concatenate([a_high, a_low], 0), h_pair)
            gram = gram + (both[:rows] + both[rows:] + dot_nt(a_high, l_pair))
        summed = jnp.where(keep[:rows] > 0.5, gram, 0.0).reshape(len(ks), NY, cols).sum(1)
        summed = jnp.concatenate([summed, jnp.zeros((4 - len(ks), cols), F32)], 0)
        s_both = jnp.concatenate(split(summed), 0)
        summed = dot_nn(s_both, of_orbital[...])
        pout[batch] = summed[:4] + summed[4:]
        sums = new(pbuf.at[batch])
        sent[7 + batch]["span"] = sums["span"]
        for k in range(NDOM):
            remote(pout.at[batch], pbuf.at[batch, dom], across(k), sums, sent[7 + batch])
        return sums

    def remove(batch, ks, copies, halves):
        rows = len(ks) * NY
        arrive(copies)
        proj = pbuf[batch].sum(0) * (1.0 / (NX * NDOM * NY * NZ))
        spread = dot_nn(jnp.concatenate(split(proj), 0), to_cells[...])
        weights = []
        for first in (0, 4):
            one = spread[first : first + len(ks)]
            one = jnp.broadcast_to(one[:, None, :], (len(ks), NY, cols)).reshape(rows, cols)
            weights.append(jnp.where(keep[:rows] > 0.5, one, 0.0).astype(BF))
        k_both = jnp.concatenate(weights, 0)
        for x, h_pair, l_pair in x_pairs():
            both = dot_nn(k_both, h_pair)
            part = both[:rows] + both[rows:] + dot_nn(weights[0], l_pair)
            for i, k in enumerate(ks):
                remo[chip(k), x] = part[i * NY : (i + 1) * NY, :NZ]
                remo[chip(k), x + 1] = part[i * NY : (i + 1) * NY, NZ:]
            if x == 2 or x == 6:
                halves(x // 4)

    phase[0] = 3
    one, on = new(), new()
    gather_one(shard, 0, one)
    gather_one(shard, 1, one)
    two = [gather_two(shard, 0), gather_two(shard, 1)]
    arrive(one)
    batches = ((0, 1, -1), (2, -2), (3, -3, 4))
    sums = [project(0, batches[0])]
    gather_on(shard, 0, two[0], on, on)
    gather_on(shard, 1, two[1], on, on)
    sums.append(project(1, batches[1]))

    def removed(k):
        return remo.at[chip(k + 4)]

    def owned(k):
        return grad.at[2 * chip(k + 4) + 1 - q]

    phase[0] = 4
    far, last, twins = [], [new(), new()], [new(), new()]
    remove(0, batches[0], sums[0], lambda h: far.append(scatter_far(removed, 1, h)))
    arrive(on)
    base = new()
    remote(shard(4), ham, sibling, base)
    sums.append(project(2, batches[2]))
    panel_copies = new(panels.at[pl.ds(0, NORB - 1)])
    sent[6]["span"] = panel_copies["span"]
    for k in range(1, NORB):
        to = lax.rem(orb + k, NORB)
        remote(packed.at[to], panels.at[orb], (dom, to), panel_copies, sent[6])
    remove(1, batches[1], sums[1], lambda h: None)
    for h in range(2):
        scatter_mid(removed, 1, h, far[h], last[h])
    remove(2, batches[2], sums[2], lambda h: scatter_near(removed, 1, h, last[h]))

    phase[0] = 5

    def to_sibling(k, h):
        ref = owned(k).at[pl.ds(4 * h, 4)]
        remote(ref, ref, sibling, twins[h])

    arrive(base)
    two, one, three, four = [], [new(), new()], [new(), new()], [new(), new()]
    for h in range(2):
        half = pl.ds(4 * h, 4)
        owned(0)[half] = ham[half] - scatter_sum(removed, 1, h, last[h])
        two.append(gather_two(owned, h))
        gather_one(owned, h, one[h])
        to_sibling(0, h)

    arrive(panel_copies)
    rows = NB * NY
    panel = panels[owner_ref[0]]
    panel = jnp.broadcast_to(panel[:, None, :], (2, 8, 128)).reshape(NB, 128)
    own = indicator((NB, 128), lambda r: r & 7, lambda c: c >> 4)
    p_both = jnp.concatenate(split(jnp.where(own, panel, 0.0)), 0)
    of_column = indicator((rows, 128), lambda r: r >> 4, lambda c: c & (NB - 1))
    by_row = dot_nt(jnp.where(of_column, 1.0, 0.0).astype(BF), p_both).astype(BF)
    to_rows = indicator((NB, rows), lambda r: r, lambda c: c >> 4)
    to_rows = jnp.where(to_rows, 1.0, 0.0).astype(BF)
    same_y = indicator((rows, rows), lambda r: r & (NY - 1), lambda c: c & (NY - 1))
    w_high, w_low = (
        jnp.where(same_y, dot_nn(one_of, to_rows), 0.0).astype(BF)
        for one_of in (by_row[:, :NB], by_row[:, NB:])
    )
    w_both = jnp.concatenate([w_high, w_low], 0)

    w_ref[...] = w_both
    upd[:, 4:] = x2[q, :, 4:]

    for h in range(2):
        gather_on(owned, h, two[h], three[h], four[h], to_sibling)
    for h in range(2):
        arrive(one[h])
        to_sibling(-1, h)
        to_sibling(1, h)
    for h in range(2):
        arrive(three[h])
        to_sibling(-3, h)
        to_sibling(3, h)
        arrive(four[h])
        to_sibling(4, h)

    arrive(twins[0])
    for x in range(0, 4, 2):
        update(grad, w_both, x2.at[q], upd, x, x)
    arrive(twins[1])
    for group in sent:
        span(group).wait_send()
    assert next(groups) == recv.shape[0]


def update(grad, w_both, old, new, x, at):
    rows = NB * NY
    g_pair = jnp.concatenate([grad[:, x].reshape(rows, NZ), grad[:, x + 1].reshape(rows, NZ)], 1)
    g_high, g_low = split(g_pair)
    both = dot_nn(w_both, g_high)
    part = both[:rows] + both[rows:] + dot_nn(w_both[:rows], g_low)
    new[:, at] = old[:, x] + part[:, :NZ].reshape(NB, NY, NZ)
    new[:, at + 1] = old[:, x + 1] + part[:, NZ:].reshape(NB, NY, NZ)


def update_kernel(grad, w_ref, upd, grad_hbm, upd_hbm, done, sem):
    outs = []

    def out(src, dst):
        outs.append(pltpu.make_async_copy(src, dst, sem.at[len(outs)]))
        outs[-1].start()

    out(upd.at[:, pl.ds(0, 4)], upd_hbm.at[:, pl.ds(0, 4)])
    out(grad, grad_hbm)
    w_both = w_ref[...]
    for x in range(4, NX, 2):
        pair = pl.ds(x, 2)
        update(grad, w_both, upd, done, x, x - 4)
        out(done.at[:, pl.ds(x - 4, 2)], upd_hbm.at[:, pair])
    for copy in outs:
        copy.wait()


def per_device(orbitals, potential, rotation, block, owner):
    shard = (NX, NY, NZ)
    scratch = [
        pltpu.VMEM((2, NB, *shard), F32),
        pltpu.VMEM((2, NB, *shard), BF),
        pltpu.VMEM((2, NB, *shard), BF),
        pltpu.VMEM(shard, F32),
        pltpu.VMEM((NB, NB * NORB), F32),
        pltpu.VMEM((NCHIP, *shard), F32),
        pltpu.VMEM((NCHIP, *shard), F32),
        pltpu.VMEM((NX + 2 * HALO, NY, NZ), F32),
        pltpu.VMEM(shard, F32),
        pltpu.VMEM((NCHIP, *shard), F32),
        pltpu.VMEM((3, 4, 128), F32),
        pltpu.VMEM((3, NDOM, 4, 128), F32),
        pltpu.VMEM((3 * NY, 2 * NB * NY), F32),
        pltpu.VMEM((2 * NB * NY, 128), BF),
        pltpu.VMEM((128, 2 * NB * NY), BF),
        pltpu.VMEM((NORB, 2, 128), F32),
        pltpu.VMEM((NORB, 2, 128), F32),
        pltpu.VMEM((2, 2, *shard), F32),
        pltpu.VMEM((2, 2, *shard), F32),
        pltpu.VMEM((2, 2, *shard), F32),
        pltpu.VMEM((2, 2, *shard), F32),
        pltpu.VMEM((2, 2, *shard), F32),
        pltpu.SemaphoreType.DMA((10,)),
        pltpu.SemaphoreType.DMA((39,)),
        pltpu.SemaphoreType.DMA((3,)),
        pltpu.SemaphoreType.REGULAR((3,)),
    ]
    hbm = pl.BlockSpec(memory_space=pl.ANY)
    smem = pl.BlockSpec(memory_space=pltpu.SMEM)
    vmem = pl.BlockSpec(memory_space=pltpu.VMEM)
    whole = jax.ShapeDtypeStruct((NB, *shard), F32)
    arrays = (pltpu.with_memory_space_constraint(v, pltpu.HBM) for v in (orbitals, potential, rotation))
    gradient, weights, updated = pl.pallas_call(
        kernel,
        out_shape=(whole, jax.ShapeDtypeStruct((2 * NB * NY, NB * NY), BF), whole),
        in_specs=[smem, smem, hbm, hbm, hbm],
        out_specs=(vmem, vmem, vmem),
        scratch_shapes=scratch,
        compiler_params=pltpu.CompilerParams(
            collective_id=0, has_side_effects=True, vmem_limit_bytes=40 << 20
        ),
        cost_estimate=pl.CostEstimate(flops=1 << 28, bytes_accessed=3 << 20, transcendentals=0),
        name="gradient",
    )(block, owner, *arrays)
    return pl.pallas_call(
        update_kernel,
        out_shape=(whole, whole),
        in_specs=[vmem, vmem, vmem],
        out_specs=(hbm, hbm),
        scratch_shapes=[
            pltpu.VMEM((NB, NX // 2, NY, NZ), F32),
            pltpu.SemaphoreType.DMA((4,)),
        ],
        compiler_params=pltpu.CompilerParams(vmem_limit_bytes=16 << 20),
        cost_estimate=pl.CostEstimate(flops=1 << 28, bytes_accessed=4 << 20, transcendentals=0),
        name="update",
    )(gradient, weights, updated)


def solution(mesh):
    in_specs = (P("orb", "dom", None, None), P("dom", None, None), P("orb", None), P(), P())
    out_specs = (P(None, "dom", None, None), P("orb", "dom", None, None))
    return jax.shard_map(
        per_device, mesh=mesh, in_specs=in_specs, out_specs=out_specs, check_vma=False
    )
```
